256 devices in a mesh: branch: 2 (over y_hi), blk: 16 (over x, y_lo, core), head: 8 (over z).
Axes of the slice: x: 4, y: 4 (y_hi: 2, y_lo: 2; y = y_hi * 2 + y_lo), z: 8, core: 2. Of those that a mesh axis runs over, the one named last changes fastest.
Arguments:
- queries: bfloat16 [2, 6144, 2048], P('branch', 'blk', 'head'), may hold values from -600 to 600
- keys: bfloat16 [2, 6144, 2048], P('branch', 'blk', 'head'), may hold values from -8 to 8
- values: bfloat16 [2, 6144, 2048], P('branch', 'blk', 'head'), may hold values from -6 to 6
- reward_grad: bfloat16 [6144, 2048], P('blk', 'head'), may hold values from -1.1953125 to 1.1953125
- qkv_weight: bfloat16 [3, 3072, 2048], P(None, None, 'head'), may hold values from -0.109375 to 0.109375
Outputs:
- latent_grad: bfloat16 [6144, 3072], P(('blk', 'head'), 'branch')
The draws below stay inside these ranges and needn't reach their ends.
All inputs are finite; a program needn't handle non-finite values.
Results may differ from the reference program's by a relative error of at most 0.02.
Values may be sent and summed in bfloat16 or wider, within the bound.
A program may use at most 128 MiB of HBM per device.

```python
import jax
import jax.numpy as jnp
from jax import lax

D = 3072
HEAD_DIM = 128
HEADS = 16
TOKENS = 6144


def query_key_pair(key, query_spread, key_spread, strength):
    first, second, third, fourth = jax.random.split(key, 4)
    shape = (2, TOKENS, HEADS * HEAD_DIM)
    query_vals = jnp.clip(jax.random.normal(first, shape, jnp.float32), -5.0, 5.0)
    key_vals = jnp.clip(jax.random.normal(second, shape, jnp.float32), -5.0, 5.0)
    query_scale = jnp.exp(jax.random.uniform(third, (2, TOKENS, 1), jnp.float32) * jnp.log(query_spread))
    key_scale = jnp.exp(jax.random.uniform(fourth, (2, TOKENS, 1), jnp.float32) * jnp.log(key_spread))
    query_vals = query_vals * query_scale
    key_vals = key_vals * key_scale
    ladder = jnp.arange(8)
    rows = ladder * (TOKENS // 8) + 5
    cols = (rows * 3 + 17) % (TOKENS - 1)
    weight = jnp.minimum(strength, 1.0)
    factor = (strength * (1.0 + ladder)).astype(jnp.float32)
    chosen = key_vals[:, cols]
    neighbour = chosen * (1.0 - 0.15 / jnp.maximum(factor, 1.0))[None, :, None]
    key_vals = key_vals.at[:, cols + 1].set(weight * neighbour + (1.0 - weight) * key_vals[:, cols + 1])
    query_vals = query_vals.at[:, rows].set((1.0 - weight) * query_vals[:, rows])
    return (query_vals, key_vals)


def draw_queries(key, part):
    pair = query_key_pair(key, 1.0, 1.0, 0.0)
    return pair[0].astype(jnp.bfloat16)


def draw_keys(key, part):
    pair = query_key_pair(key, 1.0, 1.0, 0.0)
    return pair[1].astype(jnp.bfloat16)


def with_spikes(drawn, own_key, source, target, parts, factor):
    def block_of(dim):
        return (jnp.arange(drawn.shape[dim]) // (drawn.shape[dim] // parts)).reshape((-1,) + (1,) * (drawn.ndim - 1 - dim))

    one_side = jax.random.permutation(own_key, parts)[block_of(target)]
    far = (block_of(target) + parts // 2) % parts
    return jnp.where((block_of(source) == one_side) | (block_of(source) == far), factor * drawn, drawn)


def steps_of(rng, dims, shards, least, top_value):
    def one(position, blocks):
        draws = jax.random.uniform(jax.random.fold_in(jax.random.fold_in(rng, 6), position), (blocks,), jnp.float32, least / len(shards), top_value / len(shards))
        return jnp.repeat(jnp.exp(draws), dims[position] // blocks).reshape((-1,) + (1,) * (len(dims) - position - 1))

    level = one(*shards[0])
    for cut in shards[1:]:
        level = level * one(*cut)
    return level


def normal_values(rng, shape, spread, reach, cuts=(), held_as=jnp.bfloat16):
    drawn = spread * jax.random.normal(rng, shape, jnp.float32)
    if cuts:
        drawn = drawn * steps_of(rng, shape, cuts, -0.22, 0.18)
    return jnp.clip(drawn, -reach, reach).astype(held_as)


def gaussian_with(key, extent, width, most, pieces, heavy, held_as=jnp.bfloat16):
    entries = width * jax.random.normal(key, extent, jnp.float32)
    if pieces:
        entries = entries * steps_of(key, extent, pieces, -0.22, 0.18)
    return jnp.clip(with_spikes(entries, jax.random.fold_in(key, 3), *heavy), -most, most).astype(held_as)


def setup_inputs(seed: int = 0) -> dict:
    key_list = jax.random.split(jax.random.key(seed), 6)
    queries = draw_queries(jax.random.fold_in(key_list[5], 71), 0)
    keys = draw_keys(jax.random.fold_in(key_list[5], 71), 0)
    values = normal_values(key_list[2], (2, TOKENS, HEADS * HEAD_DIM), 1.0, 6.0, ((0, 2), (1, 16), (2, 8)))
    reward_grad = normal_values(key_list[3], (TOKENS, HEADS * HEAD_DIM), 0.2, 1.1953125, ((0, 16), (1, 8)))
    qkv_weight = gaussian_with(key_list[4], (3, D, HEADS * HEAD_DIM), (3 * HEADS * HEAD_DIM) ** -0.5, 0.109375, ((2, 8),), (2, 1, 8, 2.0))
    return dict(queries=queries, keys=keys, values=values, reward_grad=reward_grad, qkv_weight=qkv_weight)


GUIDE = 6.0


def head_grads(args):
    qh, kh, vh, dh = args
    scale = HEAD_DIM ** -0.5
    scores = jnp.dot(qh, kh.T, preferred_element_type=jnp.float32) * scale
    peak = jnp.max(scores, axis=1, keepdims=True)
    lse = peak + jnp.log(jnp.sum(jnp.exp(scores - peak), axis=1, keepdims=True))
    probs = jnp.exp(scores - lse)
    attn_out = jnp.dot(probs, vh.astype(jnp.float32), precision=lax.Precision.HIGHEST)
    delta = jnp.sum(dh.astype(jnp.float32) * attn_out, axis=1, keepdims=True)
    probs_low = probs.astype(jnp.bfloat16)
    dprobs = jnp.dot(dh, vh.T, preferred_element_type=jnp.float32)
    dscores = (probs * (dprobs - delta)).astype(jnp.bfloat16)
    grad_q = jnp.dot(dscores, kh, preferred_element_type=jnp.float32) * scale
    grad_k = jnp.dot(dscores.T, qh, preferred_element_type=jnp.float32) * scale
    grad_v = jnp.dot(probs_low.T, dh, preferred_element_type=jnp.float32)
    return (grad_q.astype(jnp.bfloat16), grad_k.astype(jnp.bfloat16), grad_v.astype(jnp.bfloat16))


def by_head(array):
    return array.reshape(TOKENS, HEADS, HEAD_DIM).transpose(1, 0, 2)


def by_token(array):
    return array.transpose(1, 0, 2).reshape(TOKENS, HEADS * HEAD_DIM)


def reference(queries, keys, values, reward_grad, qkv_weight):
    total = jnp.zeros((TOKENS, D), jnp.float32)
    for side in range(2):
        coef = (1.0 - GUIDE) if side == 0 else GUIDE
        dout = (coef * reward_grad.astype(jnp.float32)).astype(jnp.bfloat16)
        grads = lax.map(head_grads, (by_head(queries[side]), by_head(keys[side]), by_head(values[side]), by_head(dout)))
        for which in range(3):
            total = total + jnp.dot(by_token(grads[which]), qkv_weight[which].T, preferred_element_type=jnp.float32)
    return total.astype(jnp.bfloat16)
```

```python
import math

import jax
import jax.numpy as jnp
from jax import lax
from jax.experimental import pallas as pl
from jax.experimental.pallas import tpu as pltpu
from jax.sharding import PartitionSpec as P

HEAD_DIM = 128
GUIDE = 6.0
MESH = pl.DeviceIdType.MESH
BF, F32 = jnp.bfloat16, jnp.float32

ROWS = 384
CHIP = 2 * ROWS
NQ = 4 * CHIP
NK = 2 * CHIP
TILE = 256
TILES = NQ // TILE
CHUNKS = NK // TILE
PER_CHIP = CHIP // TILE
FEAT = 1536
TOK = 48
SCALE = HEAD_DIM**-0.5
TO_EXP2 = SCALE * math.log2(math.e)


def dot(left, right, left_dim, right_dim):
    return lax.dot_general(
        left, right, (((left_dim,), (right_dim,)), ((), ())), preferred_element_type=F32
    )


def eights(value):
    return value.reshape(value.shape[0] // 8, 8, value.shape[1])


def kernel(
    q_in, k_in, v_in, r_in, w_in, out,
    Q, R, K, V, KT, QF, OF, E, DP, DS, SC, W, ST, SG, FD, PQ, PKV,
    XB, XS, YB, YS, BX, BR, GA, PO, ZB, ZS, FS, FR,
    q_sem, r_sem, k_sem, v_sem, g_send, w_sem, st_send, st_recv,
    x_send, x_recv, y_send, y_recv, b_send, b_recv, c_send, c_recv,
    z_send, z_recv, f_send, f_recv,
):
    branch = lax.axis_index("branch")
    blk = lax.axis_index("blk")
    z = lax.axis_index("head")
    core = lax.rem(blk, 2)
    ylo = lax.rem(blk // 2, 2)
    x = blk // 4
    y = 2 * branch + ylo
    other = 1 - core

    def device(dx=0, y_at=None, core_at=None, dz=0):
        y_to = y if y_at is None else y_at
        core_to = core if core_at is None else core_at
        x_to = lax.rem(x + dx + 4, 4)
        return (
            y_to // 2,
            (x_to * 2 + lax.rem(y_to, 2)) * 2 + core_to,
            lax.rem(z + dz + 8, 8),
        )

    y_pair = 2 * branch + (1 - ylo)
    y_far = lax.rem(y + 2, 4)
    y_up = lax.rem(y + 1, 4)
    y_down = lax.rem(y + 3, 4)
    y_rest = 2 * (1 - branch) + (1 - ylo)
    twin = device(core_at=other)

    def copy(src, dst, send, recv, to):
        return pltpu.make_async_remote_copy(
            src_ref=src, dst_ref=dst, send_sem=send, recv_sem=recv, device_id=to, device_id_type=MESH
        )

    def arrived(dst, recv):
        copy(dst, dst, recv, recv, twin).wait_recv()

    partners = [twin, device(dx=2), device(y_at=y_rest), device(y_at=y_far), device(dz=1), device(dz=-1)]
    partners += [device(y_at=y_far, core_at=other)]
    for at in (core, other):
        partners += [device(dx=1, core_at=at), device(dx=-1, core_at=at), device(y_at=y_pair, core_at=at)]
    barrier = pltpu.get_barrier_semaphore()
    for partner in partners:
        pl.semaphore_signal(barrier, inc=1, device_id=partner, device_id_type=MESH)

    mine = pl.ds(pl.multiple_of(core * HEAD_DIM, HEAD_DIM), HEAD_DIM)
    theirs = pl.ds(pl.multiple_of(other * HEAD_DIM, HEAD_DIM), HEAD_DIM)

    def rows_of(slot, half):
        return pl.ds(pl.multiple_of(slot * CHIP + half * ROWS, ROWS), ROWS)

    own = rows_of(0, core)
    local = [
        pltpu.make_async_copy(q_in.at[0, :, mine], Q.at[own], q_sem.at[0, core]),
        pltpu.make_async_copy(r_in.at[:, mine], R.at[own], r_sem.at[0, core]),
        pltpu.make_async_copy(k_in.at[0, :, mine], K.at[own], k_sem.at[0, core]),
        pltpu.make_async_copy(v_in.at[0, :, mine], V.at[own], v_sem.at[0, core]),
    ]
    for each in local:
        each.start()
    w_copy = pltpu.make_async_copy(
        w_in.at[:, pl.ds(pl.multiple_of(core * FEAT, FEAT), FEAT), :], W, w_sem
    )
    w_copy.start()
    ST[...] = jnp.zeros_like(ST)

    pl.semaphore_wait(barrier, len(partners))

    sends = []

    def send(src, dst, recv, to):
        item = copy(src, dst, g_send.at[len(sends)], recv, to)
        item.start()
        sends.append(item)

    q_of, r_of = q_in.at[0], r_in
    turn = 1 - 2 * core
    for step, (dx, slot) in enumerate(((turn, 3 - 2 * core), (-turn, 1 + 2 * core))):
        for cols, at in ((mine, core), (theirs, other)):
            to = device(dx=dx, core_at=at)
            send(q_of.at[:, cols], Q.at[rows_of(slot, core)], q_sem.at[slot, core], to)
            send(r_of.at[:, cols], R.at[rows_of(slot, core)], r_sem.at[slot, core], to)
            if step == 0:
                to = device(y_at=y_pair, core_at=at)
                send(k_in.at[0, :, cols], K.at[rows_of(1, core)], k_sem.at[1, core], to)
                send(v_in.at[0, :, cols], V.at[rows_of(1, core)], v_sem.at[1, core], to)
        if step == 0:
            send(q_of.at[:, theirs], Q.at[own], q_sem.at[0, core], twin)
            send(r_of.at[:, theirs], R.at[own], r_sem.at[0, core], twin)
            send(k_in.at[0, :, theirs], K.at[own], k_sem.at[0, core], twin)
            send(v_in.at[0, :, theirs], V.at[own], v_sem.at[0, core], twin)

    def wait_q(slot, half):
        arrived(Q.at[rows_of(slot, half)], q_sem.at[slot, half])

    def wait_r(slot, half):
        arrived(R.at[rows_of(slot, half)], r_sem.at[slot, half])

    for slot, half, dx in ((3, 0, 1), (1, 1, -1)):
        wait_q(slot, half)
        send(Q.at[rows_of(slot, half)], Q.at[rows_of(2, half)], q_sem.at[2, half], device(dx=dx))
        wait_r(slot, half)
        send(R.at[rows_of(slot, half)], R.at[rows_of(2, half)], r_sem.at[2, half], device(dx=dx))

    for each in local:
        each.wait()
    wait_q(0, other)
    wait_r(0, other)
    arrived(K.at[rows_of(0, other)], k_sem.at[0, other])
    arrived(V.at[rows_of(0, other)], v_sem.at[0, other])
    for half in range(2):
        arrived(K.at[rows_of(1, half)], k_sem.at[1, half])
        arrived(V.at[rows_of(1, half)], v_sem.at[1, half])
    for slot, half in ((3, 1), (1, 0)):
        wait_q(slot, half)
        wait_r(slot, half)
    KT[...] = K[...].T

    coef = jnp.where(branch == 0, 1.0 - GUIDE, GUIDE).astype(F32)

    def chunk(i):
        return pl.ds(i * TILE, TILE)

    def first_pass(turn, _):
        slot = jnp.where(turn < 2, turn, 5 - turn)

        @pl.when(turn == 3)
        def _():
            for half in range(2):
                wait_q(2, half)
                wait_r(2, half)
            for item in sends:
                item.wait_send()

        stat = lax.rem(x + slot, 4) * PER_CHIP

        def scores(t):
            rows = pl.ds(pl.multiple_of(slot * CHIP + t * TILE, TILE), TILE)
            q_tile = Q[rows, :]
            top = None
            for i in range(CHUNKS):
                s = dot(K[chunk(i), :], q_tile, 1, 1)
                SC[t, chunk(i), :] = s
                part = jnp.max(eights(s), axis=0)
                top = part if top is None else jnp.maximum(top, part)
            return jnp.max(top, axis=0, keepdims=True)

        def rest(t, top):
            tile = slot * PER_CHIP + t
            rows = pl.ds(pl.multiple_of(slot * CHIP + t * TILE, TILE), TILE)
            o_tile = (coef * R[rows, :].astype(F32)).astype(BF)
            OF[rows, :] = o_tile
            total, cross = jnp.zeros((8, TILE), F32), jnp.zeros((8, TILE), F32)
            for i in range(CHUNKS):
                e = jnp.exp2((SC[t, chunk(i), :] - top) * TO_EXP2)
                p = dot(V[chunk(i), :], o_tile, 1, 1)
                E[tile, chunk(i), :] = e.astype(BF)
                DP[tile, chunk(i), :] = p
                total += jnp.sum(eights(e), axis=0)
                cross += jnp.sum(eights(e * p), axis=0)
            at = pl.ds(stat + t, 1)
            ST[0, at, :] = top
            ST[1, at, :] = jnp.sum(total, axis=0, keepdims=True)
            ST[2, at, :] = jnp.sum(cross, axis=0, keepdims=True)

        tops = [scores(0)]
        for t in range(PER_CHIP):
            if t + 1 < PER_CHIP:
                tops.append(scores(t + 1))
            rest(t, tops[t])
        return 0

    lax.fori_loop(0, 4, first_pass, 0)

    stat_sends = []
    for i, dx in enumerate((2, 1, 3)):
        item = copy(ST, SG.at[i], st_send.at[i], st_recv.at[i], device(dx=dx))
        item.start()
        stat_sends.append(item)
    for item in stat_sends:
        item.wait()
    top = ST[0]
    for i in range(3):
        top = jnp.maximum(top, SG[i, 0])
    here = jnp.exp2((ST[0] - top) * TO_EXP2)
    total, cross = here * ST[1], here * ST[2]
    for i in range(3):
        fade = jnp.exp2((SG[i, 0] - top) * TO_EXP2)
        total += fade * SG[i, 1]
        cross += fade * SG[i, 2]
    FD[0] = here / total
    FD[1] = cross / total

    def second_pass(turn, _):
        slot = jnp.where(turn == 0, 2, jnp.where(turn == 1, 1, jnp.where(turn == 2, 3, 0)))
        stat = lax.rem(x + slot, 4) * PER_CHIP
        for t in range(PER_CHIP):
            tile = slot * PER_CHIP + t
            rows = pl.ds(pl.multiple_of(slot * CHIP + t * TILE, TILE), TILE)
            at = pl.ds(stat + t, 1)
            f, delta = FD[0, at, :], FD[1, at, :]
            for i in range(CHUNKS):
                ds = E[tile, chunk(i), :].astype(F32) * (DP[tile, chunk(i), :] - delta)
                DS[tile, chunk(i), :] = ds.astype(BF)
            part = dot(KT[...], DS[tile], 1, 0) * (f * SCALE)
            PQ[rows, :] = part.T.astype(BF)
            column = jnp.broadcast_to(f, (HEAD_DIM, TILE)).T
            OF[rows, :] = (OF[rows, :].astype(F32) * column).astype(BF)
            QF[rows, :] = (Q[rows, :].astype(F32) * (column * SCALE)).astype(BF)
        return 0

    lax.fori_loop(0, 4, second_pass, 0)

    class Ring:
        def __init__(self, part, landed, staged, send_sems, recv_sems, to):
            self.part, self.landed, self.staged = part, landed, staged
            self.send_sems, self.recv_sems, self.to = send_sems, recv_sems, to
            self.items = []

        def start(self, way, far, half, src):
            slot = 0 if far else 1 + half
            item = copy(
                src, self.landed.at[way, slot], self.send_sems.at[way, slot],
                self.recv_sems.at[way, slot], self.to[way],
            )
            item.start()
            self.items.append(item)

        def far(self, way):
            self.start(way, True, way, self.part(2, way))

        def plain(self, way):
            self.start(way, False, 1 - way, self.part(1 + 2 * way, 1 - way))

        def relay(self, way):
            arrived(self.landed.at[way, 0], self.recv_sems.at[way, 0])
            mid = self.part(1 + 2 * way, way)[...].astype(F32) + self.landed[way, 0].astype(F32)
            self.staged[way] = mid.astype(BF)
            self.start(way, False, way, self.staged.at[way])

        def total(self, half):
            for way in range(2):
                arrived(self.landed.at[way, 1 + half], self.recv_sems.at[way, 1 + half])
            return (
                self.part(0, half)[...].astype(F32)
                + self.landed[0, 1 + half].astype(F32)
                + self.landed[1, 1 + half].astype(F32)
            )

        def finish(self):
            for item in self.items:
                item.wait_send()

    xr = Ring(
        lambda slot, half: PQ.at[rows_of(slot, half)],
        XB, XS, x_send, x_recv, (device(dx=1), device(dx=-1)),
    )
    for way in range(2):
        xr.far(way)
        xr.plain(way)

    def third_pass(i, _):
        rows = pl.ds(pl.multiple_of(i * TILE, TILE), TILE)
        grad_v, grad_k = jnp.zeros((TILE, HEAD_DIM), F32), jnp.zeros((TILE, HEAD_DIM), F32)
        for t in range(TILES):
            grad_v += dot(E[t, rows, :], OF[chunk(t), :], 1, 0)
            grad_k += dot(DS[t, rows, :], QF[chunk(t), :], 1, 0)
        PKV[0, rows, :] = grad_v.astype(BF)
        PKV[1, rows, :] = grad_k.astype(BF)
        return 0

    lax.fori_loop(0, CHUNKS // 2, third_pass, 0)
    for way in range(2):
        xr.relay(way)
    lax.fori_loop(CHUNKS // 2, CHUNKS, third_pass, 0)

    owners = (branch, y_up // 2, 1 - branch, y_down // 2)
    yr = Ring(
        lambda slot, half: PKV.at[half, rows_of(0 if slot % 2 == 0 else 1, owners[slot])],
        YB, YS, y_send, y_recv, (device(y_at=y_up), device(y_at=y_down)),
    )
    for way in range(2):
        yr.far(way)
        yr.plain(way)

    for half in range(2):
        BX[half] = xr.total(half).astype(BF)
    cross_copy = copy(BX.at[1 - branch], BR, b_send, b_recv, device(y_at=y_far))
    cross_copy.start()
    for way in range(2):
        yr.relay(way)
    cross_copy.wait_recv()
    GA[core, 0] = (BX[branch].astype(F32) + BR[...].astype(F32)).astype(BF)
    GA[core, 2] = yr.total(0).astype(BF)
    GA[core, 1] = yr.total(1).astype(BF)
    swap = copy(GA.at[core], GA.at[core], c_send, c_recv, twin)
    swap.start()
    arrived(GA.at[other], c_recv)
    w_copy.wait()

    def project(i, _):
        feats = pl.ds(pl.multiple_of(i * TILE, TILE), TILE)
        total = jnp.zeros((ROWS, TILE), F32)
        for which in range(3):
            both = jnp.concatenate([GA[0, which], GA[1, which]], axis=1)
            total += dot(both, W[which, feats, :], 1, 1)
        PO[:, feats] = total.astype(BF)
        return 0

    lax.fori_loop(0, FEAT // TILE, project, 0)

    z_to = (device(dz=1), device(dz=-1))
    z_items = []
    width = FEAT // 2

    def z_part(way, dist, half):
        at = lax.rem(z + (dist if way == 0 else 8 - dist), 8)
        return PO.at[pl.ds(pl.multiple_of(at * TOK, 16), TOK), pl.ds(half * width, width)]

    def z_start(way, dist, half, src):
        item = copy(
            src, ZB.at[way, dist - 1, half], z_send.at[way, dist - 1, half],
            z_recv.at[way, dist - 1, half], z_to[way],
        )
        item.start()
        z_items.append(item)

    for way in range(2):
        z_start(way, 4, way, z_part(way, 4, way))
    for way in range(2):
        z_start(way, 3, 1 - way, z_part(way, 3, 1 - way))
    for dist in (3, 2, 1):
        for first in range(2):
            for way in range(2):
                half = way if first == 0 else 1 - way
                if dist == 3 and half != way:
                    continue
                arrived(ZB.at[way, dist, half], z_recv.at[way, dist, half])
                mid = z_part(way, dist, half)[...].astype(F32) + ZB[way, dist, half].astype(F32)
                ZS[way, dist - 1, half] = mid.astype(BF)
                z_start(way, dist, half, ZS.at[way, dist - 1, half])
    for half in range(2):
        for way in range(2):
            arrived(ZB.at[way, 0, half], z_recv.at[way, 0, half])
        done = (
            z_part(0, 0, half)[...].astype(F32)
            + ZB[0, 0, half].astype(F32)
            + ZB[1, 0, half].astype(F32)
        )
        FS[:, pl.ds(half * width, width)] = done.astype(BF)

    @pl.when(branch == core)
    def _():
        out[...] = FS[...]

    @pl.when(branch != core)
    def _():
        last = copy(FS, FR, f_send, f_recv, device(y_at=y_far, core_at=other))
        last.start()
        last.wait()
        out[...] = FR[...]

    xr.finish()
    yr.finish()
    cross_copy.wait_send()
    swap.wait_send()
    for item in z_items:
        item.wait_send()


def per_device(queries, keys, values, reward_grad, qkv_weight):
    def vm(*shape, dtype=BF):
        return pltpu.VMEM(shape, dtype)

    dma = pltpu.SemaphoreType.DMA
    scratch = [
        vm(NQ, HEAD_DIM), vm(NQ, HEAD_DIM), vm(NK, HEAD_DIM), vm(NK, HEAD_DIM),
        vm(HEAD_DIM, NK), vm(NQ, HEAD_DIM), vm(NQ, HEAD_DIM),
        vm(TILES, NK, TILE), vm(TILES, NK, TILE, dtype=F32), vm(TILES, NK, TILE),
        vm(PER_CHIP, NK, TILE, dtype=F32), vm(3, FEAT, 2 * HEAD_DIM),
        vm(3, 16, TILE, dtype=F32), vm(3, 3, 16, TILE, dtype=F32), vm(2, 16, TILE, dtype=F32),
        vm(NQ, HEAD_DIM), vm(2, NK, HEAD_DIM),
        vm(2, 3, ROWS, HEAD_DIM), vm(2, ROWS, HEAD_DIM),
        vm(2, 3, ROWS, HEAD_DIM), vm(2, ROWS, HEAD_DIM),
        vm(2, ROWS, HEAD_DIM), vm(ROWS, HEAD_DIM), vm(2, 3, ROWS, HEAD_DIM),
        vm(ROWS, FEAT), vm(2, 4, 2, TOK, FEAT // 2), vm(2, 3, 2, TOK, FEAT // 2),
        vm(TOK, FEAT), vm(TOK, FEAT),
        dma((4, 2)), dma((4, 2)), dma((2, 2)), dma((2, 2)), dma((20,)), dma(()),
        dma((3,)), dma((3,)), dma((2, 3)), dma((2, 3)), dma((2, 3)), dma((2, 3)),
        dma(()), dma(()), dma(()), dma(()), dma((2, 4, 2)), dma((2, 4, 2)), dma(()), dma(()),
    ]
    return pl.pallas_call(
        kernel,
        out_shape=jax.ShapeDtypeStruct((TOK, FEAT), BF),
        in_specs=[pl.BlockSpec(memory_space=pl.ANY)] * 5,
        out_specs=pl.BlockSpec(memory_space=pltpu.VMEM),
        scratch_shapes=scratch,
        compiler_params=pltpu.CompilerParams(
            collective_id=0, has_side_effects=True, vmem_limit_bytes=62 * 2**20
        ),
    )(queries, keys, values, reward_grad, qkv_weight)


def solution(mesh):
    placed = (
        P("branch", "blk", "head"),
        P("branch", "blk", "head"),
        P("branch", "blk", "head"),
        P("blk", "head"),
        P(None, None, "head"),
    )
    return jax.shard_map(
        per_device,
        mesh=mesh,
        in_specs=placed,
        out_specs=P(("blk", "head"), "branch"),
        check_vma=False,
    )
```

```python
import math

import jax
import jax.numpy as jnp
from jax import lax
from jax.experimental import pallas as pl
from jax.experimental.pallas import tpu as pltpu
from jax.sharding import PartitionSpec as P

HEAD_DIM = 128
GUIDE = 6.0
MESH = pl.DeviceIdType.MESH
BF, F32 = jnp.bfloat16, jnp.float32

ROWS = 384
CHIP = 2 * ROWS
NQ = 4 * CHIP
NK = 2 * CHIP
TILE = 256
WIDE = 1024
TILES = NQ // TILE
CHUNKS = NK // TILE
PER_CHIP = CHIP // TILE
FEAT = 1536
TOK = 48
SUBS = 1
SCALE = HEAD_DIM**-0.5
TO_EXP2 = SCALE * math.log2(math.e)


def dot(left, right, left_dim, right_dim):
    return lax.dot_general(
        left, right, (((left_dim,), (right_dim,)), ((), ())), preferred_element_type=F32
    )


def eights(value):
    return value.reshape(value.shape[0] // 8, 8, value.shape[1])


def kernel(
    q_in, k_in, v_in, r_in, w_in, out,
    Q, R, K, V, KT, QF, OG, E, DS, SC, DP, X, Y, W, ST, SG, FD, PQ, PKV,
    XB, YB, BX, BR, GA, PF, PO, ZB, ZS, ZF, ZO,
    q_sem, r_sem, k_sem, v_sem, g_send, w_sem, st_send, st_recv,
    x_send, x_recv, y_send, y_recv, b_send, b_recv, c_send, c_recv,
    z_send, z_recv, f_send, f_recv,
):
    branch = lax.axis_index("branch")
    blk = lax.axis_index("blk")
    z = lax.axis_index("head")
    core = lax.rem(blk, 2)
    ylo = lax.rem(blk // 2, 2)
    x = blk // 4
    y = 2 * branch + ylo
    other = 1 - core

    def device(dx=0, y_at=None, core_at=None, dz=0):
        y_to = y if y_at is None else y_at
        core_to = core if core_at is None else core_at
        x_to = lax.rem(x + dx + 4, 4)
        return (
            y_to // 2,
            (x_to * 2 + lax.rem(y_to, 2)) * 2 + core_to,
            lax.rem(z + dz + 8, 8),
        )

    y_pair = 2 * branch + (1 - ylo)
    y_far = lax.rem(y + 2, 4)
    y_up = lax.rem(y + 1, 4)
    y_down = lax.rem(y + 3, 4)
    y_rest = 2 * (1 - branch) + (1 - ylo)
    twin = device(core_at=other)

    def copy(src, dst, send, recv, to):
        return pltpu.make_async_remote_copy(
            src_ref=src, dst_ref=dst, send_sem=send, recv_sem=recv, device_id=to, device_id_type=MESH
        )

    def arrived(dst, recv):
        copy(dst, dst, recv, recv, twin).wait_recv()

    partners = [twin, device(y_at=y_rest), device(y_at=y_far), device(dz=1), device(dz=-1)]
    for at in (core, other):
        partners += [device(dx=1, core_at=at), device(dx=-1, core_at=at), device(y_at=y_pair, core_at=at)]
    barrier = pltpu.get_barrier_semaphore()
    for partner in partners:
        pl.semaphore_signal(barrier, inc=1, device_id=partner, device_id_type=MESH)

    mine = pl.ds(pl.multiple_of(core * HEAD_DIM, HEAD_DIM), HEAD_DIM)
    theirs = pl.ds(pl.multiple_of(other * HEAD_DIM, HEAD_DIM), HEAD_DIM)

    def rows_of(slot, half):
        return pl.ds(pl.multiple_of(slot * CHIP + half * ROWS, ROWS), ROWS)

    own = rows_of(0, core)
    local = [
        pltpu.make_async_copy(q_in.at[0, :, mine], Q.at[own], q_sem.at[0, core]),
        pltpu.make_async_copy(r_in.at[:, mine], R.at[own], r_sem.at[0, core]),
        pltpu.make_async_copy(k_in.at[0, :, mine], K.at[own], k_sem.at[0, core]),
        pltpu.make_async_copy(v_in.at[0, :, mine], V.at[own], v_sem.at[0, core]),
    ]
    for each in local:
        each.start()
    w_copy = pltpu.make_async_copy(
        w_in.at[:, pl.ds(pl.multiple_of(core * FEAT, FEAT), FEAT), :], W, w_sem
    )
    w_copy.start()
    ST[...] = jnp.zeros_like(ST)

    pl.semaphore_wait(barrier, len(partners))

    sends = []

    def send(src, dst, recv, to):
        item = copy(src, dst, g_send.at[len(sends)], recv, to)
        item.start()
        sends.append(item)

    q_of, r_of = q_in.at[0], r_in
    turn = 1 - 2 * core
    for step, (dx, slot) in enumerate(((turn, 3 - 2 * core), (-turn, 1 + 2 * core))):
        there = rows_of(slot, core)
        for cols, at in ((theirs, other), (mine, core)):
            send(q_of.at[:, cols], Q.at[there], q_sem.at[slot, core], device(dx=dx, core_at=at))
        for cols, at in ((theirs, other), (mine, core)):
            send(r_of.at[:, cols], R.at[there], r_sem.at[slot, core], device(dx=dx, core_at=at))
        if step == 0:
            there = rows_of(1, core)
            for cols, at in ((theirs, other), (mine, core)):
                to = device(y_at=y_pair, core_at=at)
                send(k_in.at[0, :, cols], K.at[there], k_sem.at[1, core], to)
                send(v_in.at[0, :, cols], V.at[there], v_sem.at[1, core], to)
            send(q_of.at[:, theirs], Q.at[own], q_sem.at[0, core], twin)
            send(r_of.at[:, theirs], R.at[own], r_sem.at[0, core], twin)
            send(k_in.at[0, :, theirs], K.at[own], k_sem.at[0, core], twin)
            send(v_in.at[0, :, theirs], V.at[own], v_sem.at[0, core], twin)

    def wait_q(slot, half):
        arrived(Q.at[rows_of(slot, half)], q_sem.at[slot, half])

    def wait_r(slot, half):
        arrived(R.at[rows_of(slot, half)], r_sem.at[slot, half])

    relays = ((3, 0, 1), (1, 1, -1))
    for slot, half, dx in relays:
        wait_q(slot, half)
        send(Q.at[rows_of(slot, half)], Q.at[rows_of(2, half)], q_sem.at[2, half], device(dx=dx))
    for slot, half, dx in relays:
        wait_r(slot, half)
        send(R.at[rows_of(slot, half)], R.at[rows_of(2, half)], r_sem.at[2, half], device(dx=dx))

    for each in local:
        each.wait()
    wait_q(0, other)
    wait_r(0, other)
    arrived(K.at[rows_of(0, other)], k_sem.at[0, other])
    arrived(V.at[rows_of(0, other)], v_sem.at[0, other])
    for half in range(2):
        arrived(K.at[rows_of(1, half)], k_sem.at[1, half])
        arrived(V.at[rows_of(1, half)], v_sem.at[1, half])
    for slot, half in ((3, 1), (1, 0)):
        wait_q(slot, half)
        wait_r(slot, half)
    KT[...] = K[...].T

    coef = jnp.where(branch == 0, 1.0 - GUIDE, GUIDE).astype(F32)

    def chunk(i):
        return pl.ds(i * TILE, TILE)

    def tile_at(slot, t):
        return pl.ds(pl.multiple_of(slot * CHIP + t * TILE, TILE), TILE)

    stat_offsets = (2, 1, 3)

    def stat_copies(chip):
        return [
            copy(ST.at[chip], SG.at[i, chip], st_send.at[i, chip], st_recv.at[i, chip], device(dx=dx))
            for i, dx in enumerate(stat_offsets)
        ]

    def first_pass(turn, _):
        slot = jnp.where(turn < 2, turn, 5 - turn)
        chip = lax.rem(x + slot, 4)

        @pl.when(turn == 3)
        def _():
            for half in range(2):
                wait_q(2, half)
                wait_r(2, half)

        def scores(t):
            q_tile = Q[tile_at(slot, t), :]
            top = None
            for i in range(CHUNKS):
                s = dot(K[chunk(i), :], q_tile, 1, 1)
                SC[t, chunk(i), :] = s
                part = jnp.max(eights(s), axis=0)
                top = part if top is None else jnp.maximum(top, part)
            return jnp.max(top, axis=0, keepdims=True)

        def sums(t, top):
            cols = tile_at(slot, t)
            o_tile = (coef * R[cols, :].astype(F32)).astype(BF)
            OG[cols, :HEAD_DIM] = o_tile
            total, cross = jnp.zeros((8, TILE), F32), jnp.zeros((8, TILE), F32)
            for i in range(CHUNKS):
                e = jnp.exp2((SC[t, chunk(i), :] - top) * TO_EXP2)
                p = dot(V[chunk(i), :], o_tile, 1, 1)
                E[chunk(i), cols] = e.astype(BF)
                SC[t, chunk(i), :] = e
                DP[t, chunk(i), :] = p
                total += jnp.sum(eights(e), axis=0)
                cross += jnp.sum(eights(e * p), axis=0)
            total = jnp.sum(total, axis=0, keepdims=True)
            cross = jnp.sum(cross, axis=0, keepdims=True)
            ST[chip, 0:1, chunk(t)] = top
            ST[chip, 1:2, chunk(t)] = total
            ST[chip, 2:3, chunk(t)] = cross
            return cross / total

        def grads(t, delta):
            cols = tile_at(slot, t)
            for i in range(CHUNKS):
                ds = SC[t, chunk(i), :] * (DP[t, chunk(i), :] - delta)
                DS[chunk(i), cols] = ds.astype(BF)

        tops = [scores(0), scores(1)]
        deltas = [sums(0, tops[0])]
        tops.append(scores(2))
        deltas.append(sums(1, tops[1]))
        grads(0, deltas[0])
        deltas.append(sums(2, tops[2]))
        for item in stat_copies(chip):
            item.start()
        grads(1, deltas[1])
        grads(2, deltas[2])
        return 0

    lax.fori_loop(0, 4, first_pass, 0)

    def key_products(i, _):
        cols = pl.ds(pl.multiple_of(i * WIDE, WIDE), WIDE)
        X[:, cols] = dot(KT[...], DS[:, cols], 1, 0)
        Y[:, cols] = dot(KT[...], E[:, cols], 1, 0)
        return 0

    lax.fori_loop(0, NQ // WIDE, key_products, 0)

    for chip in range(4):
        for item in stat_copies(chip):
            item.wait()
        top, total, cross = (ST[chip, k : k + 1, :] for k in range(3))
        whole = top
        for i in range(3):
            whole = jnp.maximum(whole, SG[i, chip, 0:1, :])
        here = jnp.exp2((top - whole) * TO_EXP2)
        total_all, cross_all = here * total, here * cross
        for i in range(3):
            fade = jnp.exp2((SG[i, chip, 0:1, :] - whole) * TO_EXP2)
            total_all += fade * SG[i, chip, 1:2, :]
            cross_all += fade * SG[i, chip, 2:3, :]
        FD[chip, 0:1, :] = here / total_all
        FD[chip, 1:2, :] = cross / total - cross_all / total_all

    def second_pass(turn, _):
        slot = jnp.where(turn == 0, 2, jnp.where(turn == 1, 1, jnp.where(turn == 2, 3, 0)))
        chip = lax.rem(x + slot, 4)
        for t in range(PER_CHIP):
            cols = tile_at(slot, t)
            f, shift = FD[chip, 0:1, chunk(t)], FD[chip, 1:2, chunk(t)]
            part = (X[:, cols] + shift * Y[:, cols]) * (f * SCALE)
            PQ[cols, :] = part.T.astype(BF)
            f_col = jnp.broadcast_to(f, (HEAD_DIM, TILE)).T
            s_col = jnp.broadcast_to(shift, (HEAD_DIM, TILE)).T
            q_tile = Q[cols, :].astype(F32) * (f_col * SCALE)
            QF[cols, :] = q_tile.astype(BF)
            OG[cols, HEAD_DIM:] = (q_tile * s_col).astype(BF)
            OG[cols, :HEAD_DIM] = (OG[cols, :HEAD_DIM].astype(F32) * f_col).astype(BF)
        return 0

    lax.fori_loop(0, 4, second_pass, 0)

    x_items = []
    for step, half in enumerate((1 - branch, branch)):
        for i, dx in enumerate((2, 1, 3)):
            item = copy(
                PQ.at[rows_of(dx, half)], XB.at[step, i], x_send.at[step, i], x_recv.at[step, i], device(dx=dx)
            )
            item.start()
            x_items.append(item)

    def y_copy(i):
        to = device(y_at=lax.rem(y + jnp.where(i == 0, 2, jnp.where(i == 1, 1, 3)), 4))
        return copy(PKV.at[i], YB.at[i], y_send.at[i], y_recv.at[i], to)

    def third_pass(i, _):
        slot = jnp.where((i == 1) | (i == 2), 1, 0)
        half = jnp.where(
            i == 0, 1 - branch, jnp.where(i == 1, y_up // 2, jnp.where(i == 2, y_down // 2, branch))
        )
        rows = rows_of(slot, half)
        both = dot(E[rows, :], OG[...], 1, 0)
        grad_k = dot(DS[rows, :], QF[...], 1, 0) + both[:, HEAD_DIM:]
        PKV[i, 0] = grad_k.astype(BF)
        PKV[i, 1] = both[:, :HEAD_DIM].astype(BF)

        @pl.when(i < 3)
        def _():
            y_copy(i).start()

        return 0

    lax.fori_loop(0, 4, third_pass, 0)

    def x_sum(step, half):
        total = PQ[rows_of(0, half), :].astype(F32)
        for i in range(3):
            arrived(XB.at[step, i], x_recv.at[step, i])
            total += XB[step, i].astype(F32)
        return total

    BX[...] = x_sum(0, 1 - branch).astype(BF)
    cross_copy = copy(BX, BR, b_send, b_recv, device(y_at=y_far))
    cross_copy.start()
    total_q = x_sum(1, branch)
    for i in range(3):
        arrived(YB.at[i], y_recv.at[i])
    for k in range(2):
        total = PKV[3, k].astype(F32)
        for i in range(3):
            total += YB[i, k].astype(F32)
        GA[core, 1 + k] = total.astype(BF)
    swap = copy(GA.at[core, pl.ds(1, 2)], GA.at[core, pl.ds(1, 2)], c_send.at[0], c_recv.at[0], twin)
    swap.start()
    cross_copy.wait_recv()
    GA[core, 0] = (total_q + BR[...].astype(F32)).astype(BF)
    swap_q = copy(GA.at[core, 0], GA.at[core, 0], c_send.at[1], c_recv.at[1], twin)
    swap_q.start()
    w_copy.wait()
    arrived(GA.at[other, pl.ds(1, 2)], c_recv.at[0])

    def both_heads(which):
        return jnp.concatenate([GA[0, which], GA[1, which]], axis=1)

    for i in range(FEAT // TILE):
        PF[:, chunk(i)] = dot(both_heads(1), W[1, chunk(i), :], 1, 1) + dot(both_heads(2), W[2, chunk(i), :], 1, 1)
    arrived(GA.at[other, 0], c_recv.at[1])
    for i in range(FEAT // TILE):
        PO[:, chunk(i)] = (PF[:, chunk(i)] + dot(both_heads(0), W[0, chunk(i), :], 1, 1)).astype(BF)

    owner_y, owner_core = 2 * core + ylo, branch
    z_to = (device(dz=1), device(dz=-1))
    end_to = tuple(device(y_at=owner_y, core_at=owner_core, dz=dz) for dz in (1, -1))
    z_items = []
    width = FEAT // 2 // SUBS

    def z_part(way, dist, half, sub):
        at = lax.rem(z + (dist if way == 0 else 8 - dist), 8)
        return PO.at[
            pl.ds(pl.multiple_of(at * TOK, 16), TOK), pl.ds((half * SUBS + sub) * width, width)
        ]

    def z_start(way, dist, half, sub, src):
        place = (way, dist - 1, half, sub)
        item = copy(
            src, ZB.at[place] if dist > 1 else ZF.at[way, half, sub], z_send.at[place], z_recv.at[place],
            z_to[way] if dist > 1 else end_to[way],
        )
        item.start()
        z_items.append(item)

    for sub in range(SUBS):
        for way in range(2):
            z_start(way, 4, way, sub, z_part(way, 4, way, sub))
    for sub in range(SUBS):
        for way in range(2):
            z_start(way, 3, 1 - way, sub, z_part(way, 3, 1 - way, sub))
    at_home = pl.ds(pl.multiple_of(z * TOK, 16), TOK)
    own_part = copy(
        PO.at[at_home], ZO, f_send, f_recv, device(y_at=y_far, core_at=other)
    )

    @pl.when(branch != core)
    def _():
        own_part.start()

    for dist, chain in ((3, 0), (2, 1), (2, 0), (1, 1), (1, 0)):
        for sub in range(SUBS):
            for way in range(2):
                half = way if chain == 0 else 1 - way
                place = (way, dist, half, sub)
                arrived(ZB.at[place], z_recv.at[place])
                mid = z_part(way, dist, half, sub)[...].astype(F32) + ZB[place].astype(F32)
                place = (way, dist - 1, half, sub)
                ZS[place] = mid.astype(BF)
                z_start(way, dist, half, sub, ZS.at[place])

    @pl.when(branch == core)
    def _():
        ZO[...] = PO[at_home, :]

    @pl.when(branch != core)
    def _():
        own_part.wait()

    for half in range(2):
        for sub in range(SUBS):
            cols = pl.ds((half * SUBS + sub) * width, width)
            done = ZO[:, cols].astype(F32)
            for way in range(2):
                arrived(ZF.at[way, half, sub], z_recv.at[way, 0, half, sub])
                done += ZF[way, half, sub].astype(F32)
            out[:, cols] = done.astype(BF)

    for item in sends:
        item.wait_send()
    for item in x_items:
        item.wait_send()
    for i in range(3):
        y_copy(i).wait_send()
    cross_copy.wait_send()
    swap.wait_send()
    swap_q.wait_send()
    for item in z_items:
        item.wait_send()


def per_device(queries, keys, values, reward_grad, qkv_weight):
    def vm(*shape, dtype=BF):
        return pltpu.VMEM(shape, dtype)

    dma = pltpu.SemaphoreType.DMA
    sub = FEAT // 2 // SUBS
    scratch = [
        vm(NQ, HEAD_DIM), vm(NQ, HEAD_DIM), vm(NK, HEAD_DIM), vm(NK, HEAD_DIM),
        vm(HEAD_DIM, NK), vm(NQ, HEAD_DIM), vm(NQ, 2 * HEAD_DIM),
        vm(NK, NQ), vm(NK, NQ),
        vm(PER_CHIP, NK, TILE, dtype=F32), vm(PER_CHIP, NK, TILE, dtype=F32),
        vm(HEAD_DIM, NQ, dtype=F32), vm(HEAD_DIM, NQ, dtype=F32),
        vm(3, FEAT, 2 * HEAD_DIM),
        vm(4, 8, CHIP, dtype=F32), vm(3, 4, 8, CHIP, dtype=F32), vm(4, 8, CHIP, dtype=F32),
        vm(NQ, HEAD_DIM), vm(4, 2, ROWS, HEAD_DIM),
        vm(2, 3, ROWS, HEAD_DIM), vm(3, 2, ROWS, HEAD_DIM),
        vm(ROWS, HEAD_DIM), vm(ROWS, HEAD_DIM), vm(2, 3, ROWS, HEAD_DIM),
        vm(ROWS, FEAT, dtype=F32), vm(ROWS, FEAT),
        vm(2, 4, 2, SUBS, TOK, sub), vm(2, 3, 2, SUBS, TOK, sub),
        vm(2, 2, SUBS, TOK, sub), vm(TOK, FEAT),
        dma((4, 2)), dma((4, 2)), dma((2, 2)), dma((2, 2)), dma((20,)), dma(()),
        dma((3, 4)), dma((3, 4)), dma((2, 3)), dma((2, 3)), dma((3,)), dma((3,)),
        dma(()), dma(()), dma((2,)), dma((2,)), dma((2, 4, 2, SUBS)), dma((2, 4, 2, SUBS)), dma(()), dma(()),
    ]
    return pl.pallas_call(
        kernel,
        out_shape=jax.ShapeDtypeStruct((TOK, FEAT), BF),
        in_specs=[pl.BlockSpec(memory_space=pl.ANY)] * 5,
        out_specs=pl.BlockSpec(memory_space=pltpu.VMEM),
        scratch_shapes=scratch,
        compiler_params=pltpu.CompilerParams(
            collective_id=0, has_side_effects=True, vmem_limit_bytes=62 * 2**20
        ),
    )(queries, keys, values, reward_grad, qkv_weight)


def solution(mesh):
    placed = (
        P("branch", "blk", "head"),
        P("branch", "blk", "head"),
        P("branch", "blk", "head"),
        P("blk", "head"),
        P(None, None, "head"),
    )
    return jax.shard_map(
        per_device,
        mesh=mesh,
        in_specs=placed,
        out_specs=P(("blk", "head"), "branch"),
        check_vma=False,
    )
```

```python
import math

import jax
import jax.numpy as jnp
from jax import lax
from jax.experimental import pallas as pl
from jax.experimental.pallas import tpu as pltpu
from jax.sharding import PartitionSpec as P

HEAD_DIM = 128
GUIDE = 6.0
MESH = pl.DeviceIdType.MESH
BF, F32 = jnp.bfloat16, jnp.float32

ROWS = 384
CHIP = 2 * ROWS
NQ = 4 * CHIP
NK = 2 * CHIP
TILE = 256
TILES = NQ // TILE
CHUNKS = NK // TILE
PER_CHIP = CHIP // TILE
FEAT = 1536
TOK = 48
SUBS = 1
SCALE = HEAD_DIM**-0.5
TO_EXP2 = SCALE * math.log2(math.e)


def dot(left, right, left_dim, right_dim):
    return lax.dot_general(
        left, right, (((left_dim,), (right_dim,)), ((), ())), preferred_element_type=F32
    )


def eights(value):
    return value.reshape(value.shape[0] // 8, 8, value.shape[1])


def kernel(
    q_in, k_in, v_in, r_in, w_in, out,
    Q, R, K, V, KT, QF, OF, E, DS, SC, DP, W, ST, SG, FD, PQ, PKV,
    XB, YB, BX, BR, GA, PF, PO, ZB, ZS, ZF, ZO,
    q_sem, r_sem, k_sem, v_sem, g_send, w_sem, st_send, st_recv,
    x_send, x_recv, y_send, y_recv, b_send, b_recv, c_send, c_recv,
    z_send, z_recv, f_send, f_recv,
):
    branch = lax.axis_index("branch")
    blk = lax.axis_index("blk")
    z = lax.axis_index("head")
    core = lax.rem(blk, 2)
    ylo = lax.rem(blk // 2, 2)
    x = blk // 4
    y = 2 * branch + ylo
    other = 1 - core

    def device(dx=0, y_at=None, core_at=None, dz=0):
        y_to = y if y_at is None else y_at
        core_to = core if core_at is None else core_at
        x_to = lax.rem(x + dx + 4, 4)
        return (
            y_to // 2,
            (x_to * 2 + lax.rem(y_to, 2)) * 2 + core_to,
            lax.rem(z + dz + 8, 8),
        )

    y_pair = 2 * branch + (1 - ylo)
    y_far = lax.rem(y + 2, 4)
    y_up = lax.rem(y + 1, 4)
    y_down = lax.rem(y + 3, 4)
    y_rest = 2 * (1 - branch) + (1 - ylo)
    twin = device(core_at=other)

    def copy(src, dst, send, recv, to):
        return pltpu.make_async_remote_copy(
            src_ref=src, dst_ref=dst, send_sem=send, recv_sem=recv, device_id=to, device_id_type=MESH
        )

    def arrived(dst, recv):
        copy(dst, dst, recv, recv, twin).wait_recv()

    partners = [twin, device(y_at=y_rest), device(y_at=y_far), device(dz=1), device(dz=-1)]
    for at in (core, other):
        partners += [device(dx=1, core_at=at), device(dx=-1, core_at=at), device(y_at=y_pair, core_at=at)]
    barrier = pltpu.get_barrier_semaphore()
    for partner in partners:
        pl.semaphore_signal(barrier, inc=1, device_id=partner, device_id_type=MESH)

    mine = pl.ds(pl.multiple_of(core * HEAD_DIM, HEAD_DIM), HEAD_DIM)
    theirs = pl.ds(pl.multiple_of(other * HEAD_DIM, HEAD_DIM), HEAD_DIM)

    def rows_of(slot, half):
        return pl.ds(pl.multiple_of(slot * CHIP + half * ROWS, ROWS), ROWS)

    own = rows_of(0, core)
    local = [
        pltpu.make_async_copy(q_in.at[0, :, mine], Q.at[own], q_sem.at[0, core]),
        pltpu.make_async_copy(r_in.at[:, mine], R.at[own], r_sem.at[0, core]),
        pltpu.make_async_copy(k_in.at[0, :, mine], K.at[own], k_sem.at[0, core]),
        pltpu.make_async_copy(v_in.at[0, :, mine], V.at[own], v_sem.at[0, core]),
    ]
    for each in local:
        each.start()
    w_copy = pltpu.make_async_copy(
        w_in.at[:, pl.ds(pl.multiple_of(core * FEAT, FEAT), FEAT), :], W, w_sem
    )
    w_copy.start()
    ST[...] = jnp.zeros_like(ST)

    pl.semaphore_wait(barrier, len(partners))

    sends = []

    def send(src, dst, recv, to):
        item = copy(src, dst, g_send.at[len(sends)], recv, to)
        item.start()
        sends.append(item)

    heads = ((theirs, other), (mine, core))
    pair = rows_of(1, core)
    for first in range(2):
        for cols, at in heads:
            for dx, slot, queries in ((1, 3, first == 0), (-1, 1, first == 1)):
                there, to = rows_of(slot, core), device(dx=dx, core_at=at)
                if queries:
                    send(q_in.at[0, :, cols], Q.at[there], q_sem.at[slot, core], to)
                else:
                    send(r_in.at[:, cols], R.at[there], r_sem.at[slot, core], to)
            to = device(y_at=y_pair, core_at=at)
            if first == 0:
                send(k_in.at[0, :, cols], K.at[pair], k_sem.at[1, core], to)
            else:
                send(v_in.at[0, :, cols], V.at[pair], v_sem.at[1, core], to)

    send(k_in.at[0, :, theirs], K.at[own], k_sem.at[0, core], twin)
    send(v_in.at[0, :, theirs], V.at[own], v_sem.at[0, core], twin)
    send(q_in.at[0, :, theirs], Q.at[own], q_sem.at[0, core], twin)
    send(r_in.at[:, theirs], R.at[own], r_sem.at[0, core], twin)

    def wait_q(slot, half):
        arrived(Q.at[rows_of(slot, half)], q_sem.at[slot, half])

    def wait_r(slot, half):
        arrived(R.at[rows_of(slot, half)], r_sem.at[slot, half])

    for half in range(2):
        wait_q(3, half)
        send(Q.at[rows_of(3, half)], Q.at[rows_of(2, half)], q_sem.at[2, half], device(dx=1))
        wait_r(1, half)
        send(R.at[rows_of(1, half)], R.at[rows_of(2, half)], r_sem.at[2, half], device(dx=-1))

    for each in local:
        each.wait()
    wait_q(0, other)
    wait_r(0, other)
    arrived(K.at[rows_of(0, other)], k_sem.at[0, other])
    arrived(V.at[rows_of(0, other)], v_sem.at[0, other])
    for half in range(2):
        arrived(K.at[rows_of(1, half)], k_sem.at[1, half])

    coef = jnp.where(branch == 0, 1.0 - GUIDE, GUIDE).astype(F32)

    def chunk(i):
        return pl.ds(i * TILE, TILE)

    def tile_at(slot, t):
        return pl.ds(pl.multiple_of(slot * CHIP + t * TILE, TILE), TILE)

    stat_offsets = (2, 1, 3)

    def stat_copies(chip):
        return [
            copy(ST.at[chip], SG.at[i, chip], st_send.at[i, chip], st_recv.at[i, chip], device(dx=dx))
            for i, dx in enumerate(stat_offsets)
        ]

    def scores(slot, t):
        q_tile = Q[tile_at(slot, t), :]
        top = None
        for i in range(CHUNKS):
            s = dot(K[chunk(i), :], q_tile, 1, 1)
            SC[t, chunk(i), :] = s
            part = jnp.max(eights(s), axis=0)
            top = part if top is None else jnp.maximum(top, part)
        return jnp.max(top, axis=0, keepdims=True)

    def sums(slot, t, top):
        chip = lax.rem(x + slot, 4)
        cols = tile_at(slot, t)
        o_tile = (coef * R[cols, :].astype(F32)).astype(BF)
        OF[cols, :] = o_tile
        total, cross = jnp.zeros((8, TILE), F32), jnp.zeros((8, TILE), F32)
        for i in range(CHUNKS):
            e = jnp.exp2((SC[t, chunk(i), :] - top) * TO_EXP2)
            p = dot(V[chunk(i), :], o_tile, 1, 1)
            E[chunk(i), cols] = e.astype(BF)
            DP[chunk(i), cols] = p
            total += jnp.sum(eights(e), axis=0)
            cross += jnp.sum(eights(e * p), axis=0)
        ST[chip, 0:1, chunk(t)] = top
        ST[chip, 1:2, chunk(t)] = jnp.sum(total, axis=0, keepdims=True)
        ST[chip, 2:3, chunk(t)] = jnp.sum(cross, axis=0, keepdims=True)

    def first_pass(turn, tops):
        slot = jnp.where(turn == 0, 0, jnp.where(turn == 1, 3, 1))
        later = jnp.where(turn == 0, 3, jnp.where(turn == 1, 1, 2))

        @pl.when(turn == 1)
        def _():
            for half in range(2):
                wait_r(3, half)
                wait_q(1, half)

        @pl.when(turn == 2)
        def _():
            for half in range(2):
                wait_q(2, half)

        new = []
        for t in range(PER_CHIP):
            sums(slot, t, tops[t])
            new.append(scores(later, t))
        for item in stat_copies(lax.rem(x + slot, 4)):
            item.start()
        return tuple(new)

    tops = tuple(scores(0, t) for t in range(PER_CHIP))
    KT[...] = K[...].T
    for half in range(2):
        arrived(V.at[rows_of(1, half)], v_sem.at[1, half])
    tops = lax.fori_loop(0, 3, first_pass, tops)
    for half in range(2):
        wait_r(2, half)
    for t in range(PER_CHIP):
        sums(2, t, tops[t])
    for item in stat_copies(lax.rem(x + 2, 4)):
        item.start()

    def x_copy(turn, step):
        slot = jnp.where(turn == 0, 2, jnp.where(turn == 1, 1, 3))
        half = 1 - branch if step == 0 else branch
        return copy(
            PQ.at[rows_of(slot, half)], XB.at[step, turn], x_send.at[step, turn], x_recv.at[step, turn],
            device(dx=slot),
        )

    def row_factors(slot):
        chip = lax.rem(x + slot, 4)
        for item in stat_copies(chip):
            item.wait_recv()
        top = ST[chip, 0:1, :]
        whole = top
        for i in range(3):
            whole = jnp.maximum(whole, SG[i, chip, 0:1, :])
        here = jnp.exp2((top - whole) * TO_EXP2)
        total_all, cross_all = here * ST[chip, 1:2, :], here * ST[chip, 2:3, :]
        for i in range(3):
            fade = jnp.exp2((SG[i, chip, 0:1, :] - whole) * TO_EXP2)
            total_all += fade * SG[i, chip, 1:2, :]
            cross_all += fade * SG[i, chip, 2:3, :]
        factor = here / total_all
        FD[slot, 0:1, :] = factor * SCALE
        FD[slot, 1:2, :] = cross_all / total_all
        for t in range(PER_CHIP):
            cols = tile_at(slot, t)
            column = jnp.broadcast_to(factor[:, t * TILE : (t + 1) * TILE], (HEAD_DIM, TILE)).T
            QF[cols, :] = (Q[cols, :].astype(F32) * (column * SCALE)).astype(BF)
            OF[cols, :] = (OF[cols, :].astype(F32) * column).astype(BF)

    def second_pass(turn):
        slot = jnp.where(turn == 0, 2, jnp.where(turn == 1, 1, jnp.where(turn == 2, 3, 0)))
        for t in range(PER_CHIP):
            cols = tile_at(slot, t)
            delta = FD[slot, 1:2, chunk(t)]
            for i in range(CHUNKS):
                ds = E[chunk(i), cols].astype(F32) * (DP[chunk(i), cols] - delta)
                DS[chunk(i), cols] = ds.astype(BF)
        block = pl.ds(pl.multiple_of(slot * CHIP, CHIP), CHIP)
        part = dot(KT[...], DS[:, block], 1, 0) * FD[slot, 0:1, :]
        PQ[block, :] = part.T.astype(BF)

    def near_factors(i, _):
        row_factors(jnp.where(i == 2, 0, 1 + 2 * i))
        return 0

    def near_second(turn, _):
        second_pass(turn)

        @pl.when(turn < 3)
        def _():
            x_copy(turn, 0).start()

        return 0

    def y_copy(i, k):
        to = device(y_at=lax.rem(y + jnp.where(i == 0, 2, jnp.where(i == 1, 1, 3)), 4))
        return copy(PKV.at[i, k], YB.at[i, k], y_send.at[i, k], y_recv.at[i, k], to)

    def third_pass(k, scores_ref, factor_ref):
        def body(i, _):
            slot = jnp.where((i == 1) | (i == 2), 1, 0)
            half = jnp.where(
                i == 0, 1 - branch, jnp.where(i == 1, y_up // 2, jnp.where(i == 2, y_down // 2, branch))
            )
            grad = dot(scores_ref[rows_of(slot, half), :], factor_ref[...], 1, 0)
            PKV[i, k] = grad.astype(BF)

            @pl.when(i < 3)
            def _():
                y_copy(i, k).start()

            return 0

        lax.fori_loop(0, 4, body, 0)

    row_factors(2)
    second_pass(0)
    x_copy(0, 0).start()
    lax.fori_loop(0, 3, near_factors, 0)
    third_pass(1, E, OF)
    lax.fori_loop(1, 4, near_second, 0)
    for turn in range(3):
        x_copy(turn, 1).start()
    third_pass(0, DS, QF)
    x_items = [x_copy(turn, step) for step in range(2) for turn in range(3)]

    def x_sum(step, half):
        total = PQ[rows_of(0, half), :].astype(F32)
        for i in range(3):
            arrived(XB.at[step, i], x_recv.at[step, i])
            total += XB[step, i].astype(F32)
        return total

    BX[...] = x_sum(0, 1 - branch).astype(BF)
    cross_copy = copy(BX, BR, b_send, b_recv, device(y_at=y_far))
    cross_copy.start()
    total_q = x_sum(1, branch)
    for k in (1, 0):
        for i in range(3):
            arrived(YB.at[i, k], y_recv.at[i, k])
        total = PKV[3, k].astype(F32)
        for i in range(3):
            total += YB[i, k].astype(F32)
        GA[core, 1 + k] = total.astype(BF)
    swap = copy(GA.at[core, pl.ds(1, 2)], GA.at[core, pl.ds(1, 2)], c_send.at[0], c_recv.at[0], twin)
    swap.start()
    cross_copy.wait_recv()
    GA[core, 0] = (total_q + BR[...].astype(F32)).astype(BF)
    swap_q = copy(GA.at[core, 0], GA.at[core, 0], c_send.at[1], c_recv.at[1], twin)
    swap_q.start()
    w_copy.wait()
    arrived(GA.at[other, pl.ds(1, 2)], c_recv.at[0])

    def both_heads(which):
        return jnp.concatenate([GA[0, which], GA[1, which]], axis=1)

    for i in range(FEAT // TILE):
        PF[:, chunk(i)] = dot(both_heads(1), W[1, chunk(i), :], 1, 1) + dot(both_heads(2), W[2, chunk(i), :], 1, 1)
    arrived(GA.at[other, 0], c_recv.at[1])
    for i in range(FEAT // TILE):
        PO[:, chunk(i)] = (PF[:, chunk(i)] + dot(both_heads(0), W[0, chunk(i), :], 1, 1)).astype(BF)

    owner_y, owner_core = 2 * core + ylo, branch
    z_to = (device(dz=1), device(dz=-1))
    end_to = tuple(device(y_at=owner_y, core_at=owner_core, dz=dz) for dz in (1, -1))
    z_items = []
    width = FEAT // 2 // SUBS

    def z_part(way, dist, half, sub):
        at = lax.rem(z + (dist if way == 0 else 8 - dist), 8)
        return PO.at[
            pl.ds(pl.multiple_of(at * TOK, 16), TOK), pl.ds((half * SUBS + sub) * width, width)
        ]

    def z_start(way, dist, half, sub, src):
        place = (way, dist - 1, half, sub)
        item = copy(
            src, ZB.at[place] if dist > 1 else ZF.at[way, half, sub], z_send.at[place], z_recv.at[place],
            z_to[way] if dist > 1 else end_to[way],
        )
        item.start()
        z_items.append(item)

    for sub in range(SUBS):
        for way in range(2):
            z_start(way, 4, way, sub, z_part(way, 4, way, sub))
    for sub in range(SUBS):
        for way in range(2):
            z_start(way, 3, 1 - way, sub, z_part(way, 3, 1 - way, sub))
    at_home = pl.ds(pl.multiple_of(z * TOK, 16), TOK)
    own_part = copy(
        PO.at[at_home], ZO, f_send, f_recv, device(y_at=y_far, core_at=other)
    )

    @pl.when(branch != core)
    def _():
        own_part.start()

    for dist, chain in ((3, 0), (2, 1), (2, 0), (1, 1), (1, 0)):
        for sub in range(SUBS):
            for way in range(2):
                half = way if chain == 0 else 1 - way
                place = (way, dist, half, sub)
                arrived(ZB.at[place], z_recv.at[place])
                mid = z_part(way, dist, half, sub)[...].astype(F32) + ZB[place].astype(F32)
                place = (way, dist - 1, half, sub)
                ZS[place] = mid.astype(BF)
                z_start(way, dist, half, sub, ZS.at[place])

    @pl.when(branch == core)
    def _():
        ZO[...] = PO[at_home, :]

    @pl.when(branch != core)
    def _():
        own_part.wait()

    for half in range(2):
        for sub in range(SUBS):
            cols = pl.ds((half * SUBS + sub) * width, width)
            done = ZO[:, cols].astype(F32)
            for way in range(2):
                arrived(ZF.at[way, half, sub], z_recv.at[way, 0, half, sub])
                done += ZF[way, half, sub].astype(F32)
            out[:, cols] = done.astype(BF)

    for item in sends:
        item.wait_send()
    for item in x_items:
        item.wait_send()
    for chip in range(4):
        for item in stat_copies(chip):
            item.wait_send()
    for i in range(3):
        for k in range(2):
            y_copy(i, k).wait_send()
    cross_copy.wait_send()
    swap.wait_send()
    swap_q.wait_send()
    for item in z_items:
        item.wait_send()


def per_device(queries, keys, values, reward_grad, qkv_weight):
    def vm(*shape, dtype=BF):
        return pltpu.VMEM(shape, dtype)

    dma = pltpu.SemaphoreType.DMA
    sub = FEAT // 2 // SUBS
    scratch = [
        vm(NQ, HEAD_DIM), vm(NQ, HEAD_DIM), vm(NK, HEAD_DIM), vm(NK, HEAD_DIM),
        vm(HEAD_DIM, NK), vm(NQ, HEAD_DIM), vm(NQ, HEAD_DIM),
        vm(NK, NQ), vm(NK, NQ),
        vm(PER_CHIP, NK, TILE, dtype=F32), vm(NK, NQ, dtype=F32),
        vm(3, FEAT, 2 * HEAD_DIM),
        vm(4, 8, CHIP, dtype=F32), vm(3, 4, 8, CHIP, dtype=F32), vm(4, 8, CHIP, dtype=F32),
        vm(NQ, HEAD_DIM), vm(4, 2, ROWS, HEAD_DIM),
        vm(2, 3, ROWS, HEAD_DIM), vm(3, 2, ROWS, HEAD_DIM),
        vm(ROWS, HEAD_DIM), vm(ROWS, HEAD_DIM), vm(2, 3, ROWS, HEAD_DIM),
        vm(ROWS, FEAT, dtype=F32), vm(ROWS, FEAT),
        vm(2, 4, 2, SUBS, TOK, sub), vm(2, 3, 2, SUBS, TOK, sub),
        vm(2, 2, SUBS, TOK, sub), vm(TOK, FEAT),
        dma((4, 2)), dma((4, 2)), dma((2, 2)), dma((2, 2)), dma((20,)), dma(()),
        dma((3, 4)), dma((3, 4)), dma((2, 3)), dma((2, 3)), dma((3, 2)), dma((3, 2)),
        dma(()), dma(()), dma((2,)), dma((2,)), dma((2, 4, 2, SUBS)), dma((2, 4, 2, SUBS)), dma(()), dma(()),
    ]
    return pl.pallas_call(
        kernel,
        out_shape=jax.ShapeDtypeStruct((TOK, FEAT), BF),
        in_specs=[pl.BlockSpec(memory_space=pl.ANY)] * 5,
        out_specs=pl.BlockSpec(memory_space=pltpu.VMEM),
        scratch_shapes=scratch,
        compiler_params=pltpu.CompilerParams(
            collective_id=0, has_side_effects=True, vmem_limit_bytes=62 * 2**20
        ),
    )(queries, keys, values, reward_grad, qkv_weight)


def solution(mesh):
    placed = (
        P("branch", "blk", "head"),
        P("branch", "blk", "head"),
        P("branch", "blk", "head"),
        P("blk", "head"),
        P(None, None, "head"),
    )
    return jax.shard_map(
        per_device,
        mesh=mesh,
        in_specs=placed,
        out_specs=P(("blk", "head"), "branch"),
        check_vma=False,
    )
```

```python
import math

import jax
import jax.numpy as jnp
from jax import lax
from jax.experimental import pallas as pl
from jax.experimental.pallas import tpu as pltpu
from jax.sharding import PartitionSpec as P

HEAD_DIM = 128
GUIDE = 6.0
MESH = pl.DeviceIdType.MESH
BF, F32 = jnp.bfloat16, jnp.float32

ROWS = 384
CHIP = 2 * ROWS
NQ = 4 * CHIP
NK = 2 * CHIP
TILE = 256
TILES = NQ // TILE
CHUNKS = NK // TILE
PER_CHIP = CHIP // TILE
FEAT = 1536
TOK = 48
SUBS = 1
SCALE = HEAD_DIM**-0.5
TO_EXP2 = SCALE * math.log2(math.e)


def dot(left, right, left_dim, right_dim):
    return lax.dot_general(
        left, right, (((left_dim,), (right_dim,)), ((), ())), preferred_element_type=F32
    )


def eights(value):
    return value.reshape(value.shape[0] // 8, 8, value.shape[1])


def kernel(
    q_in, k_in, v_in, r_in, w_in, out,
    Q, R, K, V, KT, QF, OF, E, DS, SC, DP, W, ST, SG, FD, PQ, PKV,
    XB, YB, BX, BR, GA, PF, PO, ZB, ZS, ZF, ZO,
    q_sem, r_sem, k_sem, v_sem, g_send, w_sem, st_send, st_recv,
    x_send, x_recv, y_send, y_recv, b_send, b_recv, c_send, c_recv,
    z_send, z_recv, f_send, f_recv,
):
    branch = lax.axis_index("branch")
    blk = lax.axis_index("blk")
    z = lax.axis_index("head")
    core = lax.rem(blk, 2)
    ylo = lax.rem(blk // 2, 2)
    x = blk // 4
    y = 2 * branch + ylo
    other = 1 - core

    def device(dx=0, y_at=None, core_at=None, dz=0):
        y_to = y if y_at is None else y_at
        core_to = core if core_at is None else core_at
        x_to = lax.rem(x + dx + 4, 4)
        return (
            y_to // 2,
            (x_to * 2 + lax.rem(y_to, 2)) * 2 + core_to,
            lax.rem(z + dz + 8, 8),
        )

    y_pair = 2 * branch + (1 - ylo)
    y_far = lax.rem(y + 2, 4)
    y_up = lax.rem(y + 1, 4)
    y_down = lax.rem(y + 3, 4)
    y_rest = 2 * (1 - branch) + (1 - ylo)
    twin = device(core_at=other)

    def copy(src, dst, send, recv, to):
        return pltpu.make_async_remote_copy(
            src_ref=src, dst_ref=dst, send_sem=send, recv_sem=recv, device_id=to, device_id_type=MESH
        )

    def arrived(dst, recv):
        copy(dst, dst, recv, recv, twin).wait_recv()

    partners = [twin, device(y_at=y_rest), device(y_at=y_far), device(dz=1), device(dz=-1)]
    for at in (core, other):
        partners += [device(dx=1, core_at=at), device(dx=-1, core_at=at), device(y_at=y_pair, core_at=at)]
    barrier = pltpu.get_barrier_semaphore()
    for partner in partners:
        pl.semaphore_signal(barrier, inc=1, device_id=partner, device_id_type=MESH)

    mine = pl.ds(pl.multiple_of(core * HEAD_DIM, HEAD_DIM), HEAD_DIM)
    theirs = pl.ds(pl.multiple_of(other * HEAD_DIM, HEAD_DIM), HEAD_DIM)

    def rows_of(slot, half):
        return pl.ds(pl.multiple_of(slot * CHIP + half * ROWS, ROWS), ROWS)

    own = rows_of(0, core)
    local = [
        pltpu.make_async_copy(q_in.at[0, :, mine], Q.at[own], q_sem.at[0, core]),
        pltpu.make_async_copy(r_in.at[:, mine], R.at[own], r_sem.at[0, core]),
        pltpu.make_async_copy(k_in.at[0, :, mine], K.at[own], k_sem.at[0, core]),
        pltpu.make_async_copy(v_in.at[0, :, mine], V.at[own], v_sem.at[0, core]),
    ]
    for each in local:
        each.start()
    w_copy = pltpu.make_async_copy(
        w_in.at[:, pl.ds(pl.multiple_of(core * FEAT, FEAT), FEAT), :], W, w_sem
    )
    w_copy.start()
    ST[...] = jnp.zeros_like(ST)

    pl.semaphore_wait(barrier, len(partners))

    sends = []

    def send(src, dst, recv, to):
        item = copy(src, dst, g_send.at[len(sends)], recv, to)
        item.start()
        sends.append(item)

    heads = ((theirs, other), (mine, core))
    pair = rows_of(1, core)
    for first in range(2):
        for cols, at in heads:
            for dx, slot, queries in ((1, 3, first == 0), (-1, 1, first == 1)):
                there, to = rows_of(slot, core), device(dx=dx, core_at=at)
                if queries:
                    send(q_in.at[0, :, cols], Q.at[there], q_sem.at[slot, core], to)
                else:
                    send(r_in.at[:, cols], R.at[there], r_sem.at[slot, core], to)
            to = device(y_at=y_pair, core_at=at)
            if first == 0:
                send(k_in.at[0, :, cols], K.at[pair], k_sem.at[1, core], to)
            else:
                send(v_in.at[0, :, cols], V.at[pair], v_sem.at[1, core], to)

    send(k_in.at[0, :, theirs], K.at[own], k_sem.at[0, core], twin)
    send(v_in.at[0, :, theirs], V.at[own], v_sem.at[0, core], twin)
    send(q_in.at[0, :, theirs], Q.at[own], q_sem.at[0, core], twin)
    send(r_in.at[:, theirs], R.at[own], r_sem.at[0, core], twin)

    def wait_q(slot, half):
        arrived(Q.at[rows_of(slot, half)], q_sem.at[slot, half])

    def wait_r(slot, half):
        arrived(R.at[rows_of(slot, half)], r_sem.at[slot, half])

    for half in range(2):
        wait_q(3, half)
        send(Q.at[rows_of(3, half)], Q.at[rows_of(2, half)], q_sem.at[2, half], device(dx=1))
        wait_r(1, half)
        send(R.at[rows_of(1, half)], R.at[rows_of(2, half)], r_sem.at[2, half], device(dx=-1))

    for each in local:
        each.wait()
    wait_q(0, other)
    wait_r(0, other)
    arrived(K.at[rows_of(0, other)], k_sem.at[0, other])
    arrived(V.at[rows_of(0, other)], v_sem.at[0, other])
    for half in range(2):
        arrived(K.at[rows_of(1, half)], k_sem.at[1, half])

    coef = jnp.where(branch == 0, 1.0 - GUIDE, GUIDE).astype(F32)

    def chunk(i):
        return pl.ds(i * TILE, TILE)

    def tile_at(slot, t):
        return pl.ds(pl.multiple_of(slot * CHIP + t * TILE, TILE), TILE)

    stat_offsets = (2, 1, 3)

    def stat_copies(chip):
        return [
            copy(ST.at[chip], SG.at[i, chip], st_send.at[i, chip], st_recv.at[i, chip], device(dx=dx))
            for i, dx in enumerate(stat_offsets)
        ]

    def scores(slot, t):
        q_tile = Q[tile_at(slot, t), :]
        top = None
        for i in range(CHUNKS):
            s = dot(K[chunk(i), :], q_tile, 1, 1)
            SC[t, chunk(i), :] = s
            part = jnp.max(eights(s), axis=0)
            top = part if top is None else jnp.maximum(top, part)
        return jnp.max(top, axis=0, keepdims=True)

    def sums(slot, t, top):
        chip = lax.rem(x + slot, 4)
        cols = tile_at(slot, t)
        o_tile = (coef * R[cols, :].astype(F32)).astype(BF)
        OF[cols, :] = o_tile
        total, cross = jnp.zeros((8, TILE), F32), jnp.zeros((8, TILE), F32)
        for i in range(CHUNKS):
            e = jnp.exp2((SC[t, chunk(i), :] - top) * TO_EXP2)
            p = dot(V[chunk(i), :], o_tile, 1, 1)
            E[chunk(i), cols] = e.astype(BF)
            DP[chunk(i), cols] = p
            total += jnp.sum(eights(e), axis=0)
            cross += jnp.sum(eights(e * p), axis=0)
        ST[chip, 0:1, chunk(t)] = top
        ST[chip, 1:2, chunk(t)] = jnp.sum(total, axis=0, keepdims=True)
        ST[chip, 2:3, chunk(t)] = jnp.sum(cross, axis=0, keepdims=True)

    def first_pass(turn, tops):
        slot = jnp.where(turn == 0, 0, jnp.where(turn == 1, 3, 1))
        later = jnp.where(turn == 0, 3, jnp.where(turn == 1, 1, 2))

        @pl.when(turn == 1)
        def _():
            for half in range(2):
                wait_r(3, half)
                wait_q(1, half)

        @pl.when(turn == 2)
        def _():
            for half in range(2):
                wait_q(2, half)

        new = []
        for t in range(PER_CHIP):
            sums(slot, t, tops[t])
            new.append(scores(later, t))
        for item in stat_copies(lax.rem(x + slot, 4)):
            item.start()
        return tuple(new)

    tops = tuple(scores(0, t) for t in range(PER_CHIP))
    KT[...] = K[...].T
    for half in range(2):
        arrived(V.at[rows_of(1, half)], v_sem.at[1, half])
    tops = lax.fori_loop(0, 3, first_pass, tops)
    for half in range(2):
        wait_r(2, half)
    for t in range(PER_CHIP):
        sums(2, t, tops[t])
    for item in stat_copies(lax.rem(x + 2, 4)):
        item.start()

    def x_copy(turn, step):
        slot = jnp.where(turn == 0, 2, jnp.where(turn == 1, 1, 3))
        half = 1 - branch if step == 0 else branch
        return copy(
            PQ.at[rows_of(slot, half)], XB.at[step, turn], x_send.at[step, turn], x_recv.at[step, turn],
            device(dx=slot),
        )

    def row_factors(slot):
        chip = lax.rem(x + slot, 4)
        for item in stat_copies(chip):
            item.wait_recv()
        top = ST[chip, 0:1, :]
        whole = top
        for i in range(3):
            whole = jnp.maximum(whole, SG[i, chip, 0:1, :])
        here = jnp.exp2((top - whole) * TO_EXP2)
        total_all, cross_all = here * ST[chip, 1:2, :], here * ST[chip, 2:3, :]
        for i in range(3):
            fade = jnp.exp2((SG[i, chip, 0:1, :] - whole) * TO_EXP2)
            total_all += fade * SG[i, chip, 1:2, :]
            cross_all += fade * SG[i, chip, 2:3, :]
        factor = here / total_all
        FD[slot, 0:1, :] = factor * SCALE
        FD[slot, 1:2, :] = cross_all / total_all
        for t in range(PER_CHIP):
            cols = tile_at(slot, t)
            column = jnp.broadcast_to(factor[:, t * TILE : (t + 1) * TILE], (HEAD_DIM, TILE)).T
            QF[cols, :] = (Q[cols, :].astype(F32) * (column * SCALE)).astype(BF)
            OF[cols, :] = (OF[cols, :].astype(F32) * column).astype(BF)

    def second_pass(turn):
        slot = jnp.where(turn == 0, 2, jnp.where(turn == 1, 1, jnp.where(turn == 2, 3, 0)))
        for t in range(PER_CHIP):
            cols = tile_at(slot, t)
            delta = FD[slot, 1:2, chunk(t)]
            for i in range(CHUNKS):
                ds = E[chunk(i), cols].astype(F32) * (DP[chunk(i), cols] - delta)
                DS[chunk(i), cols] = ds.astype(BF)
        block = pl.ds(pl.multiple_of(slot * CHIP, CHIP), CHIP)
        part = dot(KT[...], DS[:, block], 1, 0) * FD[slot, 0:1, :]
        PQ[block, :] = part.T.astype(BF)

    def near_factors(i, _):
        row_factors(jnp.where(i == 2, 0, 1 + 2 * i))
        return 0

    def y_copy(i, k):
        to = device(y_at=lax.rem(y + jnp.where(i == 0, 2, jnp.where(i == 1, 1, 3)), 4))
        return copy(PKV.at[i, k], YB.at[i, k], y_send.at[i, k], y_recv.at[i, k], to)

    def third_pass(k, scores_ref, factor_ref, i):
        slot = jnp.where((i == 1) | (i == 2), 1, 0)
        half = jnp.where(
            i == 0, 1 - branch, jnp.where(i == 1, y_up // 2, jnp.where(i == 2, y_down // 2, branch))
        )
        grad = dot(scores_ref[rows_of(slot, half), :], factor_ref[...], 1, 0)
        PKV[i, k] = grad.astype(BF)

        @pl.when(i < 3)
        def _():
            y_copy(i, k).start()

    def alternate(i, _):
        third_pass(1, E, OF, i)

        @pl.when(i < 3)
        def _():
            second_pass(i + 1)

        @pl.when(i < 2)
        def _():
            x_copy(i + 1, 0).start()

        return 0

    def keys_part(i, _):
        third_pass(0, DS, QF, i)

        @pl.when(i == 0)
        def _():
            BX[...] = x_sum(0, 1 - branch).astype(BF)
            cross_copy.start()

        return 0

    def x_sum(step, half):
        total = PQ[rows_of(0, half), :].astype(F32)
        for i in range(3):
            arrived(XB.at[step, i], x_recv.at[step, i])
            total += XB[step, i].astype(F32)
        return total

    cross_copy = copy(BX, BR, b_send, b_recv, device(y_at=y_far))
    row_factors(2)
    second_pass(0)
    x_copy(0, 0).start()
    lax.fori_loop(0, 3, near_factors, 0)
    lax.fori_loop(0, 4, alternate, 0)
    for turn in range(3):
        x_copy(turn, 1).start()
    lax.fori_loop(0, 4, keys_part, 0)
    x_items = [x_copy(turn, step) for step in range(2) for turn in range(3)]
    total_q = x_sum(1, branch)
    for k in (1, 0):
        for i in range(3):
            arrived(YB.at[i, k], y_recv.at[i, k])
        total = PKV[3, k].astype(F32)
        for i in range(3):
            total += YB[i, k].astype(F32)
        GA[core, 1 + k] = total.astype(BF)
    swap = copy(GA.at[core, pl.ds(1, 2)], GA.at[core, pl.ds(1, 2)], c_send.at[0], c_recv.at[0], twin)
    swap.start()
    cross_copy.wait_recv()
    GA[core, 0] = (total_q + BR[...].astype(F32)).astype(BF)
    swap_q = copy(GA.at[core, 0], GA.at[core, 0], c_send.at[1], c_recv.at[1], twin)
    swap_q.start()
    w_copy.wait()
    arrived(GA.at[other, pl.ds(1, 2)], c_recv.at[0])

    def both_heads(which):
        return jnp.concatenate([GA[0, which], GA[1, which]], axis=1)

    for i in range(FEAT // TILE):
        PF[:, chunk(i)] = dot(both_heads(1), W[1, chunk(i), :], 1, 1) + dot(both_heads(2), W[2, chunk(i), :], 1, 1)
    arrived(GA.at[other, 0], c_recv.at[1])
    for i in range(FEAT // TILE):
        PO[:, chunk(i)] = (PF[:, chunk(i)] + dot(both_heads(0), W[0, chunk(i), :], 1, 1)).astype(BF)

    owner_y, owner_core = 2 * core + ylo, branch
    z_to = (device(dz=1), device(dz=-1))
    end_to = tuple(device(y_at=owner_y, core_at=owner_core, dz=dz) for dz in (1, -1))
    z_items = []
    width = FEAT // 2 // SUBS

    def z_part(way, dist, half, sub):
        at = lax.rem(z + (dist if way == 0 else 8 - dist), 8)
        return PO.at[
            pl.ds(pl.multiple_of(at * TOK, 16), TOK), pl.ds((half * SUBS + sub) * width, width)
        ]

    def z_start(way, dist, half, sub, src):
        place = (way, dist - 1, half, sub)
        item = copy(
            src, ZB.at[place] if dist > 1 else ZF.at[way, half, sub], z_send.at[place], z_recv.at[place],
            z_to[way] if dist > 1 else end_to[way],
        )
        item.start()
        z_items.append(item)

    for sub in range(SUBS):
        for way in range(2):
            z_start(way, 4, way, sub, z_part(way, 4, way, sub))
    for sub in range(SUBS):
        for way in range(2):
            z_start(way, 3, 1 - way, sub, z_part(way, 3, 1 - way, sub))
    at_home = pl.ds(pl.multiple_of(z * TOK, 16), TOK)
    own_part = copy(
        PO.at[at_home], ZO, f_send, f_recv, device(y_at=y_far, core_at=other)
    )

    @pl.when(branch != core)
    def _():
        own_part.start()

    for dist, chain in ((3, 0), (2, 1), (2, 0), (1, 1), (1, 0)):
        for sub in range(SUBS):
            for way in range(2):
                half = way if chain == 0 else 1 - way
                place = (way, dist, half, sub)
                arrived(ZB.at[place], z_recv.at[place])
                mid = z_part(way, dist, half, sub)[...].astype(F32) + ZB[place].astype(F32)
                place = (way, dist - 1, half, sub)
                ZS[place] = mid.astype(BF)
                z_start(way, dist, half, sub, ZS.at[place])

    @pl.when(branch == core)
    def _():
        ZO[...] = PO[at_home, :]

    @pl.when(branch != core)
    def _():
        own_part.wait()

    for half in range(2):
        for sub in range(SUBS):
            cols = pl.ds((half * SUBS + sub) * width, width)
            done = ZO[:, cols].astype(F32)
            for way in range(2):
                arrived(ZF.at[way, half, sub], z_recv.at[way, 0, half, sub])
                done += ZF[way, half, sub].astype(F32)
            out[:, cols] = done.astype(BF)

    for item in sends:
        item.wait_send()
    for item in x_items:
        item.wait_send()
    for chip in range(4):
        for item in stat_copies(chip):
            item.wait_send()
    for i in range(3):
        for k in range(2):
            y_copy(i, k).wait_send()
    cross_copy.wait_send()
    swap.wait_send()
    swap_q.wait_send()
    for item in z_items:
        item.wait_send()


def per_device(queries, keys, values, reward_grad, qkv_weight):
    def vm(*shape, dtype=BF):
        return pltpu.VMEM(shape, dtype)

    dma = pltpu.SemaphoreType.DMA
    sub = FEAT // 2 // SUBS
    scratch = [
        vm(NQ, HEAD_DIM), vm(NQ, HEAD_DIM), vm(NK, HEAD_DIM), vm(NK, HEAD_DIM),
        vm(HEAD_DIM, NK), vm(NQ, HEAD_DIM), vm(NQ, HEAD_DIM),
        vm(NK, NQ), vm(NK, NQ),
        vm(PER_CHIP, NK, TILE, dtype=F32), vm(NK, NQ, dtype=F32),
        vm(3, FEAT, 2 * HEAD_DIM),
        vm(4, 8, CHIP, dtype=F32), vm(3, 4, 8, CHIP, dtype=F32), vm(4, 8, CHIP, dtype=F32),
        vm(NQ, HEAD_DIM), vm(4, 2, ROWS, HEAD_DIM),
        vm(2, 3, ROWS, HEAD_DIM), vm(3, 2, ROWS, HEAD_DIM),
        vm(ROWS, HEAD_DIM), vm(ROWS, HEAD_DIM), vm(2, 3, ROWS, HEAD_DIM),
        vm(ROWS, FEAT, dtype=F32), vm(ROWS, FEAT),
        vm(2, 4, 2, SUBS, TOK, sub), vm(2, 3, 2, SUBS, TOK, sub),
        vm(2, 2, SUBS, TOK, sub), vm(TOK, FEAT),
        dma((4, 2)), dma((4, 2)), dma((2, 2)), dma((2, 2)), dma((20,)), dma(()),
        dma((3, 4)), dma((3, 4)), dma((2, 3)), dma((2, 3)), dma((3, 2)), dma((3, 2)),
        dma(()), dma(()), dma((2,)), dma((2,)), dma((2, 4, 2, SUBS)), dma((2, 4, 2, SUBS)), dma(()), dma(()),
    ]
    return pl.pallas_call(
        kernel,
        out_shape=jax.ShapeDtypeStruct((TOK, FEAT), BF),
        in_specs=[pl.BlockSpec(memory_space=pl.ANY)] * 5,
        out_specs=pl.BlockSpec(memory_space=pltpu.VMEM),
        scratch_shapes=scratch,
        compiler_params=pltpu.CompilerParams(
            collective_id=0, has_side_effects=True, vmem_limit_bytes=62 * 2**20
        ),
    )(queries, keys, values, reward_grad, qkv_weight)


def solution(mesh):
    placed = (
        P("branch", "blk", "head"),
        P("branch", "blk", "head"),
        P("branch", "blk", "head"),
        P("blk", "head"),
        P(None, None, "head"),
    )
    return jax.shard_map(
        per_device,
        mesh=mesh,
        in_specs=placed,
        out_specs=P(("blk", "head"), "branch"),
        check_vma=False,
    )
```

```python
import math

import jax
import jax.numpy as jnp
from jax import lax
from jax.experimental import pallas as pl
from jax.experimental.pallas import tpu as pltpu
from jax.sharding import PartitionSpec as P

HEAD_DIM = 128
GUIDE = 6.0
MESH = pl.DeviceIdType.MESH
BF, F32 = jnp.bfloat16, jnp.float32

ROWS = 384
CHIP = 2 * ROWS
NQ = 4 * CHIP
NK = 2 * CHIP
TILE = 256
TILES = NQ // TILE
CHUNKS = NK // TILE
PER_CHIP = CHIP // TILE
FEAT = 1536
TOK = 48
SUBS = 1
SCALE = HEAD_DIM**-0.5
TO_EXP2 = SCALE * math.log2(math.e)


def dot(left, right, left_dim, right_dim):
    return lax.dot_general(
        left, right, (((left_dim,), (right_dim,)), ((), ())), preferred_element_type=F32
    )


def eights(value):
    return value.reshape(value.shape[0] // 8, 8, value.shape[1])


def kernel(
    q_in, k_in, v_in, r_in, w_in, out,
    Q, R, K, V, KT, QF, OF, E, DS, SC, DP, W, ST, SG, FD, PQ, PKV,
    XB, YB, BX, BR, GA, PF, PO, ZB, ZS, ZF, ZO,
    q_sem, r_sem, k_sem, v_sem, g_send, w_sem, st_send, st_recv,
    x_send, x_recv, y_send, y_recv, b_send, b_recv, c_send, c_recv,
    z_send, z_recv, f_send, f_recv, far_sem,
):
    branch = lax.axis_index("branch")
    blk = lax.axis_index("blk")
    z = lax.axis_index("head")
    core = lax.rem(blk, 2)
    ylo = lax.rem(blk // 2, 2)
    x = blk // 4
    y = 2 * branch + ylo
    other = 1 - core

    def device(dx=0, y_at=None, core_at=None, dz=0):
        y_to = y if y_at is None else y_at
        core_to = core if core_at is None else core_at
        x_to = lax.rem(x + dx + 4, 4)
        return (
            y_to // 2,
            (x_to * 2 + lax.rem(y_to, 2)) * 2 + core_to,
            lax.rem(z + dz + 8, 8),
        )

    y_pair = 2 * branch + (1 - ylo)
    y_far = lax.rem(y + 2, 4)
    y_up = lax.rem(y + 1, 4)
    y_down = lax.rem(y + 3, 4)
    y_rest = 2 * (1 - branch) + (1 - ylo)
    twin = device(core_at=other)

    def copy(src, dst, send, recv, to):
        return pltpu.make_async_remote_copy(
            src_ref=src, dst_ref=dst, send_sem=send, recv_sem=recv, device_id=to, device_id_type=MESH
        )

    def arrived(dst, recv):
        copy(dst, dst, recv, recv, twin).wait_recv()

    partners = [twin, device(y_at=y_rest), device(dz=1), device(dz=-1)]
    for at in (core, other):
        partners += [device(dx=1, core_at=at), device(dx=-1, core_at=at), device(y_at=y_pair, core_at=at)]
    barrier = pltpu.get_barrier_semaphore()
    for partner in partners:
        pl.semaphore_signal(barrier, inc=1, device_id=partner, device_id_type=MESH)

    mine = pl.ds(pl.multiple_of(core * HEAD_DIM, HEAD_DIM), HEAD_DIM)
    theirs = pl.ds(pl.multiple_of(other * HEAD_DIM, HEAD_DIM), HEAD_DIM)

    def rows_of(slot, half):
        return pl.ds(pl.multiple_of(slot * CHIP + half * ROWS, ROWS), ROWS)

    own = rows_of(0, core)
    local = [
        pltpu.make_async_copy(q_in.at[0, :, mine], Q.at[own], q_sem.at[0, core]),
        pltpu.make_async_copy(r_in.at[:, mine], R.at[own], r_sem.at[0, core]),
        pltpu.make_async_copy(k_in.at[0, :, mine], K.at[own], k_sem.at[0, core]),
        pltpu.make_async_copy(v_in.at[0, :, mine], V.at[own], v_sem.at[0, core]),
    ]
    for each in local:
        each.start()
    w_copy = pltpu.make_async_copy(
        w_in.at[:, pl.ds(pl.multiple_of(core * FEAT, FEAT), FEAT), :], W, w_sem
    )
    w_copy.start()
    ST[...] = jnp.zeros_like(ST)

    pl.semaphore_wait(barrier, len(partners))
    pl.semaphore_signal(far_sem, inc=1, device_id=device(y_at=y_rest), device_id_type=MESH)

    sends = []

    def send(src, dst, recv, to):
        item = copy(src, dst, g_send.at[len(sends)], recv, to)
        item.start()
        sends.append(item)

    heads = ((theirs, other), (mine, core))
    pair = rows_of(1, core)
    for first in range(2):
        for cols, at in heads:
            for dx, slot, queries in ((1, 3, first == 0), (-1, 1, first == 1)):
                there, to = rows_of(slot, core), device(dx=dx, core_at=at)
                if queries:
                    send(q_in.at[0, :, cols], Q.at[there], q_sem.at[slot, core], to)
                else:
                    send(r_in.at[:, cols], R.at[there], r_sem.at[slot, core], to)
            to = device(y_at=y_pair, core_at=at)
            if first == 0:
                send(k_in.at[0, :, cols], K.at[pair], k_sem.at[1, core], to)
            else:
                send(v_in.at[0, :, cols], V.at[pair], v_sem.at[1, core], to)

    send(k_in.at[0, :, theirs], K.at[own], k_sem.at[0, core], twin)
    send(v_in.at[0, :, theirs], V.at[own], v_sem.at[0, core], twin)
    send(q_in.at[0, :, theirs], Q.at[own], q_sem.at[0, core], twin)
    send(r_in.at[:, theirs], R.at[own], r_sem.at[0, core], twin)

    def wait_q(slot, half):
        arrived(Q.at[rows_of(slot, half)], q_sem.at[slot, half])

    def wait_r(slot, half):
        arrived(R.at[rows_of(slot, half)], r_sem.at[slot, half])

    for half in range(2):
        wait_q(3, half)
        send(Q.at[rows_of(3, half)], Q.at[rows_of(2, half)], q_sem.at[2, half], device(dx=1))
        wait_r(1, half)
        send(R.at[rows_of(1, half)], R.at[rows_of(2, half)], r_sem.at[2, half], device(dx=-1))

    for each in local:
        each.wait()
    wait_q(0, other)
    wait_r(0, other)
    arrived(K.at[rows_of(0, other)], k_sem.at[0, other])
    arrived(V.at[rows_of(0, other)], v_sem.at[0, other])
    for half in range(2):
        arrived(K.at[rows_of(1, half)], k_sem.at[1, half])

    coef = jnp.where(branch == 0, 1.0 - GUIDE, GUIDE).astype(F32)

    def chunk(i):
        return pl.ds(i * TILE, TILE)

    def tile_at(slot, t):
        return pl.ds(pl.multiple_of(slot * CHIP + t * TILE, TILE), TILE)

    stat_offsets = (2, 1, 3)

    def stat_copies(chip):
        return [
            copy(ST.at[chip], SG.at[i, chip], st_send.at[i, chip], st_recv.at[i, chip], device(dx=dx))
            for i, dx in enumerate(stat_offsets)
        ]

    def scores(slot, t):
        q_tile = Q[tile_at(slot, t), :]
        top = None
        for i in range(CHUNKS):
            s = dot(K[chunk(i), :], q_tile, 1, 1)
            SC[t, chunk(i), :] = s
            part = jnp.max(eights(s), axis=0)
            top = part if top is None else jnp.maximum(top, part)
        return jnp.max(top, axis=0, keepdims=True)

    def sums(slot, t, top):
        chip = lax.rem(x + slot, 4)
        cols = tile_at(slot, t)
        o_tile = (coef * R[cols, :].astype(F32)).astype(BF)
        OF[cols, :] = o_tile
        total, cross = jnp.zeros((8, TILE), F32), jnp.zeros((8, TILE), F32)
        for i in range(CHUNKS):
            e = jnp.exp2((SC[t, chunk(i), :] - top) * TO_EXP2)
            p = dot(V[chunk(i), :], o_tile, 1, 1)
            E[chunk(i), cols] = e.astype(BF)
            DP[chunk(i), cols] = p
            total += jnp.sum(eights(e), axis=0)
            cross += jnp.sum(eights(e * p), axis=0)
        ST[chip, 0:1, chunk(t)] = top
        ST[chip, 1:2, chunk(t)] = jnp.sum(total, axis=0, keepdims=True)
        ST[chip, 2:3, chunk(t)] = jnp.sum(cross, axis=0, keepdims=True)

    def first_pass(turn, tops):
        slot = jnp.where(turn == 0, 0, jnp.where(turn == 1, 3, 1))
        later = jnp.where(turn == 0, 3, jnp.where(turn == 1, 1, 2))

        @pl.when(turn == 1)
        def _():
            for half in range(2):
                wait_r(3, half)
                wait_q(1, half)

        @pl.when(turn == 2)
        def _():
            for half in range(2):
                wait_q(2, half)

        new = []
        for t in range(PER_CHIP):
            sums(slot, t, tops[t])
            new.append(scores(later, t))
        for item in stat_copies(lax.rem(x + slot, 4)):
            item.start()
        return tuple(new)

    tops = tuple(scores(0, t) for t in range(PER_CHIP))
    KT[...] = K[...].T
    for half in range(2):
        arrived(V.at[rows_of(1, half)], v_sem.at[1, half])
    tops = lax.fori_loop(0, 3, first_pass, tops)
    for half in range(2):
        wait_r(2, half)
    for t in range(PER_CHIP):
        sums(2, t, tops[t])
    for item in stat_copies(lax.rem(x + 2, 4)):
        item.start()

    def x_copy(turn, step):
        slot = jnp.where(turn == 0, 2, jnp.where(turn == 1, 1, 3))
        half = 1 - branch if step == 0 else branch
        return copy(
            PQ.at[rows_of(slot, half)], XB.at[step, turn], x_send.at[step, turn], x_recv.at[step, turn],
            device(dx=slot),
        )

    def row_factors(slot):
        chip = lax.rem(x + slot, 4)
        for item in stat_copies(chip):
            item.wait_recv()
        top = ST[chip, 0:1, :]
        whole = top
        for i in range(3):
            whole = jnp.maximum(whole, SG[i, chip, 0:1, :])
        here = jnp.exp2((top - whole) * TO_EXP2)
        total_all, cross_all = here * ST[chip, 1:2, :], here * ST[chip, 2:3, :]
        for i in range(3):
            fade = jnp.exp2((SG[i, chip, 0:1, :] - whole) * TO_EXP2)
            total_all += fade * SG[i, chip, 1:2, :]
            cross_all += fade * SG[i, chip, 2:3, :]
        factor = here / total_all
        FD[slot, 0:1, :] = factor * SCALE
        FD[slot, 1:2, :] = cross_all / total_all
        for t in range(PER_CHIP):
            cols = tile_at(slot, t)
            column = jnp.broadcast_to(factor[:, t * TILE : (t + 1) * TILE], (HEAD_DIM, TILE)).T
            QF[cols, :] = (Q[cols, :].astype(F32) * (column * SCALE)).astype(BF)
            OF[cols, :] = (OF[cols, :].astype(F32) * column).astype(BF)

    def second_pass(turn):
        slot = jnp.where(turn == 0, 2, jnp.where(turn == 1, 1, jnp.where(turn == 2, 3, 0)))
        for t in range(PER_CHIP):
            cols = tile_at(slot, t)
            delta = FD[slot, 1:2, chunk(t)]
            for i in range(CHUNKS):
                ds = E[chunk(i), cols].astype(F32) * (DP[chunk(i), cols] - delta)
                DS[chunk(i), cols] = ds.astype(BF)
        block = pl.ds(pl.multiple_of(slot * CHIP, CHIP), CHIP)
        part = dot(KT[...], DS[:, block], 1, 0) * FD[slot, 0:1, :]
        PQ[block, :] = part.T.astype(BF)

    def near_factors(i, _):
        row_factors(jnp.where(i == 2, 0, 1 + 2 * i))
        return 0

    def y_copy(i, k):
        to = device(y_at=lax.rem(y + jnp.where(i == 0, 2, jnp.where(i == 1, 1, 3)), 4))
        return copy(PKV.at[i, k], YB.at[i, k], y_send.at[i, k], y_recv.at[i, k], to)

    def third_pass(k, scores_ref, factor_ref, i):
        slot = jnp.where((i == 1) | (i == 2), 1, 0)
        half = jnp.where(
            i == 0, 1 - branch, jnp.where(i == 1, y_up // 2, jnp.where(i == 2, y_down // 2, branch))
        )
        grad = dot(scores_ref[rows_of(slot, half), :], factor_ref[...], 1, 0)
        PKV[i, k] = grad.astype(BF)

        @pl.when(i < 3)
        def _():
            y_copy(i, k).start()

    def alternate(i, _):
        third_pass(1, E, OF, i)

        @pl.when(i < 3)
        def _():
            second_pass(i + 1)

        @pl.when(i < 2)
        def _():
            x_copy(i + 1, 0).start()

        return 0

    def keys_part(i, _):
        third_pass(0, DS, QF, i)

        @pl.when(i == 1)
        def _():
            BX[...] = x_sum(0, 1 - branch).astype(BF)
            cross_copy.start()

        return 0

    def x_sum(step, half):
        total = PQ[rows_of(0, half), :].astype(F32)
        for i in range(3):
            arrived(XB.at[step, i], x_recv.at[step, i])
            total += XB[step, i].astype(F32)
        return total

    cross_copy = copy(BX, BR, b_send, b_recv, device(y_at=y_far))
    row_factors(2)
    second_pass(0)
    x_copy(0, 0).start()
    lax.fori_loop(0, 3, near_factors, 0)
    pl.semaphore_wait(far_sem, 1)
    lax.fori_loop(0, 4, alternate, 0)
    for turn in range(3):
        x_copy(turn, 1).start()
    lax.fori_loop(0, 4, keys_part, 0)
    x_items = [x_copy(turn, step) for step in range(2) for turn in range(3)]
    total_q = x_sum(1, branch)
    for k in (1, 0):
        for i in range(3):
            arrived(YB.at[i, k], y_recv.at[i, k])
        total = PKV[3, k].astype(F32)
        for i in range(3):
            total += YB[i, k].astype(F32)
        GA[core, 1 + k] = total.astype(BF)
    swap = copy(GA.at[core, pl.ds(1, 2)], GA.at[core, pl.ds(1, 2)], c_send.at[0], c_recv.at[0], twin)
    swap.start()
    cross_copy.wait_recv()
    GA[core, 0] = (total_q + BR[...].astype(F32)).astype(BF)
    swap_q = copy(GA.at[core, 0], GA.at[core, 0], c_send.at[1], c_recv.at[1], twin)
    swap_q.start()
    w_copy.wait()
    arrived(GA.at[other, pl.ds(1, 2)], c_recv.at[0])

    def both_heads(which):
        return jnp.concatenate([GA[0, which], GA[1, which]], axis=1)

    for i in range(FEAT // TILE):
        PF[:, chunk(i)] = dot(both_heads(1), W[1, chunk(i), :], 1, 1) + dot(both_heads(2), W[2, chunk(i), :], 1, 1)
    arrived(GA.at[other, 0], c_recv.at[1])
    for i in range(FEAT // TILE):
        PO[:, chunk(i)] = (PF[:, chunk(i)] + dot(both_heads(0), W[0, chunk(i), :], 1, 1)).astype(BF)

    owner_y, owner_core = 2 * core + ylo, branch
    z_to = (device(dz=1), device(dz=-1))
    end_to = tuple(device(y_at=owner_y, core_at=owner_core, dz=dz) for dz in (1, -1))
    z_items = []
    width = FEAT // 2 // SUBS

    def z_part(way, dist, half, sub):
        at = lax.rem(z + (dist if way == 0 else 8 - dist), 8)
        return PO.at[
            pl.ds(pl.multiple_of(at * TOK, 16), TOK), pl.ds((half * SUBS + sub) * width, width)
        ]

    def z_start(way, dist, half, sub, src):
        place = (way, dist - 1, half, sub)
        item = copy(
            src, ZB.at[place] if dist > 1 else ZF.at[way, half, sub], z_send.at[place], z_recv.at[place],
            z_to[way] if dist > 1 else end_to[way],
        )
        item.start()
        z_items.append(item)

    for sub in range(SUBS):
        for way in range(2):
            z_start(way, 4, way, sub, z_part(way, 4, way, sub))
    for sub in range(SUBS):
        for way in range(2):
            z_start(way, 3, 1 - way, sub, z_part(way, 3, 1 - way, sub))
    at_home = pl.ds(pl.multiple_of(z * TOK, 16), TOK)
    own_part = copy(
        PO.at[at_home], ZO, f_send, f_recv, device(y_at=y_far, core_at=other)
    )

    @pl.when(branch != core)
    def _():
        own_part.start()

    for dist, chain in ((3, 0), (2, 1), (2, 0), (1, 1), (1, 0)):
        for sub in range(SUBS):
            for way in range(2):
                half = way if chain == 0 else 1 - way
                place = (way, dist, half, sub)
                arrived(ZB.at[place], z_recv.at[place])
                mid = z_part(way, dist, half, sub)[...].astype(F32) + ZB[place].astype(F32)
                place = (way, dist - 1, half, sub)
                ZS[place] = mid.astype(BF)
                z_start(way, dist, half, sub, ZS.at[place])

    @pl.when(branch == core)
    def _():
        ZO[...] = PO[at_home, :]

    @pl.when(branch != core)
    def _():
        own_part.wait()

    for half in range(2):
        for sub in range(SUBS):
            cols = pl.ds((half * SUBS + sub) * width, width)
            done = ZO[:, cols].astype(F32)
            for way in range(2):
                arrived(ZF.at[way, half, sub], z_recv.at[way, 0, half, sub])
                done += ZF[way, half, sub].astype(F32)
            out[:, cols] = done.astype(BF)

    for item in sends:
        item.wait_send()
    for item in x_items:
        item.wait_send()
    for chip in range(4):
        for item in stat_copies(chip):
            item.wait_send()
    for i in range(3):
        for k in range(2):
            y_copy(i, k).wait_send()
    cross_copy.wait_send()
    swap.wait_send()
    swap_q.wait_send()
    for item in z_items:
        item.wait_send()


def per_device(queries, keys, values, reward_grad, qkv_weight):
    def vm(*shape, dtype=BF):
        return pltpu.VMEM(shape, dtype)

    dma = pltpu.SemaphoreType.DMA
    sub = FEAT // 2 // SUBS
    scratch = [
        vm(NQ, HEAD_DIM), vm(NQ, HEAD_DIM), vm(NK, HEAD_DIM), vm(NK, HEAD_DIM),
        vm(HEAD_DIM, NK), vm(NQ, HEAD_DIM), vm(NQ, HEAD_DIM),
        vm(NK, NQ), vm(NK, NQ),
        vm(PER_CHIP, NK, TILE, dtype=F32), vm(NK, NQ, dtype=F32),
        vm(3, FEAT, 2 * HEAD_DIM),
        vm(4, 8, CHIP, dtype=F32), vm(3, 4, 8, CHIP, dtype=F32), vm(4, 8, CHIP, dtype=F32),
        vm(NQ, HEAD_DIM), vm(4, 2, ROWS, HEAD_DIM),
        vm(2, 3, ROWS, HEAD_DIM), vm(3, 2, ROWS, HEAD_DIM),
        vm(ROWS, HEAD_DIM), vm(ROWS, HEAD_DIM), vm(2, 3, ROWS, HEAD_DIM),
        vm(ROWS, FEAT, dtype=F32), vm(ROWS, FEAT),
        vm(2, 4, 2, SUBS, TOK, sub), vm(2, 3, 2, SUBS, TOK, sub),
        vm(2, 2, SUBS, TOK, sub), vm(TOK, FEAT),
        dma((4, 2)), dma((4, 2)), dma((2, 2)), dma((2, 2)), dma((20,)), dma(()),
        dma((3, 4)), dma((3, 4)), dma((2, 3)), dma((2, 3)), dma((3, 2)), dma((3, 2)),
        dma(()), dma(()), dma((2,)), dma((2,)), dma((2, 4, 2, SUBS)), dma((2, 4, 2, SUBS)), dma(()), dma(()),
        pltpu.SemaphoreType.REGULAR,
    ]
    return pl.pallas_call(
        kernel,
        out_shape=jax.ShapeDtypeStruct((TOK, FEAT), BF),
        in_specs=[pl.BlockSpec(memory_space=pl.ANY)] * 5,
        out_specs=pl.BlockSpec(memory_space=pltpu.VMEM),
        scratch_shapes=scratch,
        compiler_params=pltpu.CompilerParams(
            collective_id=0, has_side_effects=True, vmem_limit_bytes=62 * 2**20
        ),
    )(queries, keys, values, reward_grad, qkv_weight)


def solution(mesh):
    placed = (
        P("branch", "blk", "head"),
        P("branch", "blk", "head"),
        P("branch", "blk", "head"),
        P("blk", "head"),
        P(None, None, "head"),
    )
    return jax.shard_map(
        per_device,
        mesh=mesh,
        in_specs=placed,
        out_specs=P(("blk", "head"), "branch"),
        check_vma=False,
    )
```

```python
import math

import jax
import jax.numpy as jnp
from jax import lax
from jax.experimental import pallas as pl
from jax.experimental.pallas import tpu as pltpu
from jax.sharding import PartitionSpec as P

HEAD_DIM = 128
GUIDE = 6.0
MESH = pl.DeviceIdType.MESH
BF, F32 = jnp.bfloat16, jnp.float32

ROWS = 384
CHIP = 2 * ROWS
NQ = 4 * CHIP
NK = 2 * CHIP
TILE = 256
TILES = NQ // TILE
CHUNKS = NK // TILE
PER_CHIP = CHIP // TILE
FEAT = 1536
TOK = 48
SUBS = 1
SCALE = HEAD_DIM**-0.5
TO_EXP2 = SCALE * math.log2(math.e)


def dot(left, right, left_dim, right_dim):
    return lax.dot_general(
        left, right, (((left_dim,), (right_dim,)), ((), ())), preferred_element_type=F32
    )


def eights(value):
    return value.reshape(value.shape[0] // 8, 8, value.shape[1])


def kernel(
    q_in, k_in, v_in, r_in, w_in, out,
    Q, R, K, V, KT, QF, OF, E, DS, SC, DP, W, ST, SG, FD, PQ, PKV,
    XB, YB, BX, BR, GA, PF, PO, ZB, ZS, ZF, ZO,
    q_sem, r_sem, k_sem, v_sem, g_send, w_sem, st_send, st_recv,
    x_send, x_recv, y_send, y_recv, b_send, b_recv, c_send, c_recv,
    z_send, z_recv, f_send, f_recv, far_sem,
):
    branch = lax.axis_index("branch")
    blk = lax.axis_index("blk")
    z = lax.axis_index("head")
    core = lax.rem(blk, 2)
    ylo = lax.rem(blk // 2, 2)
    x = blk // 4
    y = 2 * branch + ylo
    other = 1 - core

    def device(dx=0, y_at=None, core_at=None, dz=0):
        y_to = y if y_at is None else y_at
        core_to = core if core_at is None else core_at
        x_to = lax.rem(x + dx + 4, 4)
        return (
            y_to // 2,
            (x_to * 2 + lax.rem(y_to, 2)) * 2 + core_to,
            lax.rem(z + dz + 8, 8),
        )

    y_pair = 2 * branch + (1 - ylo)
    y_far = lax.rem(y + 2, 4)
    y_up = lax.rem(y + 1, 4)
    y_down = lax.rem(y + 3, 4)
    y_rest = 2 * (1 - branch) + (1 - ylo)
    twin = device(core_at=other)

    def copy(src, dst, send, recv, to):
        return pltpu.make_async_remote_copy(
            src_ref=src, dst_ref=dst, send_sem=send, recv_sem=recv, device_id=to, device_id_type=MESH
        )

    def arrived(dst, recv):
        copy(dst, dst, recv, recv, twin).wait_recv()

    partners = [twin, device(y_at=y_rest), device(dz=1), device(dz=-1)]
    for at in (core, other):
        partners += [device(dx=1, core_at=at), device(dx=-1, core_at=at), device(y_at=y_pair, core_at=at)]
    barrier = pltpu.get_barrier_semaphore()
    for partner in partners:
        pl.semaphore_signal(barrier, inc=1, device_id=partner, device_id_type=MESH)

    mine = pl.ds(pl.multiple_of(core * HEAD_DIM, HEAD_DIM), HEAD_DIM)
    theirs = pl.ds(pl.multiple_of(other * HEAD_DIM, HEAD_DIM), HEAD_DIM)

    def rows_of(slot, half):
        return pl.ds(pl.multiple_of(slot * CHIP + half * ROWS, ROWS), ROWS)

    own = rows_of(0, core)
    local = [
        pltpu.make_async_copy(q_in.at[0, :, mine], Q.at[own], q_sem.at[0, core]),
        pltpu.make_async_copy(r_in.at[:, mine], R.at[own], r_sem.at[0, core]),
        pltpu.make_async_copy(k_in.at[0, :, mine], K.at[own], k_sem.at[0, core]),
        pltpu.make_async_copy(v_in.at[0, :, mine], V.at[own], v_sem.at[0, core]),
    ]
    for each in local:
        each.start()
    w_copy = pltpu.make_async_copy(
        w_in.at[:, pl.ds(pl.multiple_of(core * FEAT, FEAT), FEAT), :], W, w_sem
    )
    w_copy.start()
    ST[...] = jnp.zeros_like(ST)

    pl.semaphore_wait(barrier, len(partners))
    pl.semaphore_signal(far_sem, inc=1, device_id=device(y_at=y_rest), device_id_type=MESH)

    sends = []

    def send(src, dst, recv, to):
        item = copy(src, dst, g_send.at[len(sends)], recv, to)
        item.start()
        sends.append(item)

    heads = ((theirs, other), (mine, core))
    pair = rows_of(1, core)
    for first in range(2):
        for cols, at in heads:
            for dx, slot, queries in ((1, 3, first == 0), (-1, 1, first == 1)):
                there, to = rows_of(slot, core), device(dx=dx, core_at=at)
                if queries:
                    send(q_in.at[0, :, cols], Q.at[there], q_sem.at[slot, core], to)
                else:
                    send(r_in.at[:, cols], R.at[there], r_sem.at[slot, core], to)
            to = device(y_at=y_pair, core_at=at)
            if first == 0:
                send(k_in.at[0, :, cols], K.at[pair], k_sem.at[1, core], to)
            else:
                send(v_in.at[0, :, cols], V.at[pair], v_sem.at[1, core], to)

    send(k_in.at[0, :, theirs], K.at[own], k_sem.at[0, core], twin)
    send(v_in.at[0, :, theirs], V.at[own], v_sem.at[0, core], twin)
    send(q_in.at[0, :, theirs], Q.at[own], q_sem.at[0, core], twin)
    send(r_in.at[:, theirs], R.at[own], r_sem.at[0, core], twin)

    def wait_q(slot, half):
        arrived(Q.at[rows_of(slot, half)], q_sem.at[slot, half])

    def wait_r(slot, half):
        arrived(R.at[rows_of(slot, half)], r_sem.at[slot, half])

    for half in range(2):
        wait_q(3, half)
        send(Q.at[rows_of(3, half)], Q.at[rows_of(2, half)], q_sem.at[2, half], device(dx=1))
        wait_r(1, half)
        send(R.at[rows_of(1, half)], R.at[rows_of(2, half)], r_sem.at[2, half], device(dx=-1))

    for each in local:
        each.wait()
    wait_q(0, other)
    wait_r(0, other)
    arrived(K.at[rows_of(0, other)], k_sem.at[0, other])
    arrived(V.at[rows_of(0, other)], v_sem.at[0, other])
    for half in range(2):
        arrived(K.at[rows_of(1, half)], k_sem.at[1, half])

    coef = jnp.where(branch == 0, 1.0 - GUIDE, GUIDE).astype(F32)

    def chunk(i):
        return pl.ds(i * TILE, TILE)

    def tile_at(slot, t):
        return pl.ds(pl.multiple_of(slot * CHIP + t * TILE, TILE), TILE)

    stat_offsets = (2, 1, 3)

    def stat_copies(chip):
        return [
            copy(ST.at[chip], SG.at[i, chip], st_send.at[i, chip], st_recv.at[i, chip], device(dx=dx))
            for i, dx in enumerate(stat_offsets)
        ]

    def scores(slot, t):
        q_tile = Q[tile_at(slot, t), :]
        top = None
        for i in range(CHUNKS):
            s = dot(K[chunk(i), :], q_tile, 1, 1)
            SC[t, chunk(i), :] = s
            part = jnp.max(eights(s), axis=0)
            top = part if top is None else jnp.maximum(top, part)
        return jnp.max(top, axis=0, keepdims=True)

    def sums(slot, t, top):
        chip = lax.rem(x + slot, 4)
        cols = tile_at(slot, t)
        o_tile = (coef * R[cols, :].astype(F32)).astype(BF)
        OF[cols, :] = o_tile
        total, cross = jnp.zeros((8, TILE), F32), jnp.zeros((8, TILE), F32)
        for i in range(CHUNKS):
            e = jnp.exp2((SC[t, chunk(i), :] - top) * TO_EXP2)
            p = dot(V[chunk(i), :], o_tile, 1, 1)
            E[chunk(i), cols] = e.astype(BF)
            DP[chunk(i), cols] = p
            total += jnp.sum(eights(e), axis=0)
            cross += jnp.sum(eights(e * p), axis=0)
        ST[chip, 0:1, chunk(t)] = top
        ST[chip, 1:2, chunk(t)] = jnp.sum(total, axis=0, keepdims=True)
        ST[chip, 2:3, chunk(t)] = jnp.sum(cross, axis=0, keepdims=True)

    def first_pass(turn, tops):
        slot = jnp.where(turn == 0, 0, jnp.where(turn == 1, 3, 1))
        later = jnp.where(turn == 0, 3, jnp.where(turn == 1, 1, 2))

        @pl.when(turn == 1)
        def _():
            for half in range(2):
                wait_r(3, half)
                wait_q(1, half)

        @pl.when(turn == 2)
        def _():
            for half in range(2):
                wait_q(2, half)

        new = []
        for t in range(PER_CHIP):
            sums(slot, t, tops[t])
            new.append(scores(later, t))
        for item in stat_copies(lax.rem(x + slot, 4)):
            item.start()
        return tuple(new)

    tops = tuple(scores(0, t) for t in range(PER_CHIP))
    KT[...] = K[...].T
    for half in range(2):
        arrived(V.at[rows_of(1, half)], v_sem.at[1, half])
    tops = lax.fori_loop(0, 3, first_pass, tops)
    for half in range(2):
        wait_r(2, half)
    for t in range(PER_CHIP):
        sums(2, t, tops[t])
    for item in stat_copies(lax.rem(x + 2, 4)):
        item.start()

    def x_copy(turn, step):
        slot = jnp.where(turn == 0, 2, jnp.where(turn == 1, 1, 3))
        half = 1 - branch if step == 0 else branch
        return copy(
            PQ.at[rows_of(slot, half)], XB.at[step, turn], x_send.at[step, turn], x_recv.at[step, turn],
            device(dx=slot),
        )

    def row_factors(slot):
        chip = lax.rem(x + slot, 4)
        for item in stat_copies(chip):
            item.wait_recv()
        top = ST[chip, 0:1, :]
        whole = top
        for i in range(3):
            whole = jnp.maximum(whole, SG[i, chip, 0:1, :])
        here = jnp.exp2((top - whole) * TO_EXP2)
        total_all, cross_all = here * ST[chip, 1:2, :], here * ST[chip, 2:3, :]
        for i in range(3):
            fade = jnp.exp2((SG[i, chip, 0:1, :] - whole) * TO_EXP2)
            total_all += fade * SG[i, chip, 1:2, :]
            cross_all += fade * SG[i, chip, 2:3, :]
        factor = here / total_all
        FD[slot, 0:1, :] = factor * SCALE
        FD[slot, 1:2, :] = cross_all / total_all
        for t in range(PER_CHIP):
            cols = tile_at(slot, t)
            column = jnp.broadcast_to(factor[:, t * TILE : (t + 1) * TILE], (HEAD_DIM, TILE)).T
            QF[cols, :] = (Q[cols, :].astype(F32) * (column * SCALE)).astype(BF)
            OF[cols, :] = (OF[cols, :].astype(F32) * column).astype(BF)

    def second_pass(turn):
        slot = jnp.where(turn == 0, 2, jnp.where(turn == 1, 1, jnp.where(turn == 2, 3, 0)))
        for t in range(PER_CHIP):
            cols = tile_at(slot, t)
            delta = FD[slot, 1:2, chunk(t)]
            for i in range(CHUNKS):
                ds = E[chunk(i), cols].astype(F32) * (DP[chunk(i), cols] - delta)
                DS[chunk(i), cols] = ds.astype(BF)
        block = pl.ds(pl.multiple_of(slot * CHIP, CHIP), CHIP)
        part = dot(KT[...], DS[:, block], 1, 0) * FD[slot, 0:1, :]
        PQ[block, :] = part.T.astype(BF)

    def near_factors(i, _):
        row_factors(jnp.where(i == 2, 0, 1 + 2 * i))
        return 0

    def y_copy(i, k):
        to = device(y_at=lax.rem(y + jnp.where(i == 0, 2, jnp.where(i == 1, 1, 3)), 4))
        return copy(PKV.at[i, k], YB.at[i, k], y_send.at[i, k], y_recv.at[i, k], to)

    def third_pass(k, scores_ref, factor_ref, i):
        slot = jnp.where((i == 1) | (i == 2), 1, 0)
        half = jnp.where(
            i == 0, 1 - branch, jnp.where(i == 1, y_up // 2, jnp.where(i == 2, y_down // 2, branch))
        )
        grad = dot(scores_ref[rows_of(slot, half), :], factor_ref[...], 1, 0)
        PKV[i, k] = grad.astype(BF)

        @pl.when(i < 3)
        def _():
            y_copy(i, k).start()

    def alternate(i, _):
        third_pass(1, E, OF, i)

        @pl.when(i < 3)
        def _():
            second_pass(i + 1)

        @pl.when(i < 2)
        def _():
            x_copy(i + 1, 0).start()

        return 0

    def keys_part(i, _):
        third_pass(0, DS, QF, i)

        @pl.when(i == 1)
        def _():
            BX[...] = x_sum(0, 1 - branch).astype(BF)
            cross_copy.start()

        return 0

    def x_sum(step, half):
        total = PQ[rows_of(0, half), :].astype(F32)
        for i in range(3):
            arrived(XB.at[step, i], x_recv.at[step, i])
            total += XB[step, i].astype(F32)
        return total

    cross_copy = copy(BX, BR, b_send, b_recv, device(y_at=y_far))
    row_factors(2)
    second_pass(0)
    x_copy(0, 0).start()
    lax.fori_loop(0, 3, near_factors, 0)
    pl.semaphore_wait(far_sem, 1)
    lax.fori_loop(0, 4, alternate, 0)
    for turn in range(3):
        x_copy(turn, 1).start()
    lax.fori_loop(0, 4, keys_part, 0)
    x_items = [x_copy(turn, step) for step in range(2) for turn in range(3)]
    total_q = x_sum(1, branch)
    for k in (1, 0):
        for i in range(3):
            arrived(YB.at[i, k], y_recv.at[i, k])
        total = PKV[3, k].astype(F32)
        for i in range(3):
            total += YB[i, k].astype(F32)
        GA[core, 1 + k] = total.astype(BF)
    swap = copy(GA.at[core, pl.ds(1, 2)], GA.at[core, pl.ds(1, 2)], c_send.at[0], c_recv.at[0], twin)
    swap.start()
    cross_copy.wait_recv()
    GA[core, 0] = (total_q + BR[...].astype(F32)).astype(BF)
    swap_q = copy(GA.at[core, 0], GA.at[core, 0], c_send.at[1], c_recv.at[1], twin)
    swap_q.start()
    w_copy.wait()
    arrived(GA.at[other, pl.ds(1, 2)], c_recv.at[0])

    def both_heads(which):
        return jnp.concatenate([GA[0, which], GA[1, which]], axis=1)

    for i in range(FEAT // TILE):
        PF[:, chunk(i)] = dot(both_heads(1), W[1, chunk(i), :], 1, 1) + dot(both_heads(2), W[2, chunk(i), :], 1, 1)
    arrived(GA.at[other, 0], c_recv.at[1])

    owner_y, owner_core = 2 * core + ylo, branch
    z_to = (device(dz=1), device(dz=-1))
    end_to = tuple(device(y_at=owner_y, core_at=owner_core, dz=dz) for dz in (1, -1))
    z_items = []
    width = FEAT // 2 // SUBS

    def z_part(way, dist, half, sub):
        at = lax.rem(z + (dist if way == 0 else 8 - dist), 8)
        return PO.at[
            pl.ds(pl.multiple_of(at * TOK, 16), TOK), pl.ds((half * SUBS + sub) * width, width)
        ]

    def z_start(way, dist, half, sub, src):
        place = (way, dist - 1, half, sub)
        item = copy(
            src, ZB.at[place] if dist > 1 else ZF.at[way, half, sub], z_send.at[place], z_recv.at[place],
            z_to[way] if dist > 1 else end_to[way],
        )
        item.start()
        z_items.append(item)

    for way in range(2):
        for i in range(way * FEAT // TILE // 2, (way + 1) * FEAT // TILE // 2):
            PO[:, chunk(i)] = (PF[:, chunk(i)] + dot(both_heads(0), W[0, chunk(i), :], 1, 1)).astype(BF)
        for sub in range(SUBS):
            z_start(way, 4, way, sub, z_part(way, 4, way, sub))
    for sub in range(SUBS):
        for way in range(2):
            z_start(way, 3, 1 - way, sub, z_part(way, 3, 1 - way, sub))
    at_home = pl.ds(pl.multiple_of(z * TOK, 16), TOK)
    own_part = copy(
        PO.at[at_home], ZO, f_send, f_recv, device(y_at=y_far, core_at=other)
    )

    @pl.when(branch != core)
    def _():
        own_part.start()

    for dist, chain in ((3, 0), (2, 1), (2, 0), (1, 1), (1, 0)):
        for sub in range(SUBS):
            for way in range(2):
                half = way if chain == 0 else 1 - way
                place = (way, dist, half, sub)
                arrived(ZB.at[place], z_recv.at[place])
                mid = z_part(way, dist, half, sub)[...].astype(F32) + ZB[place].astype(F32)
                place = (way, dist - 1, half, sub)
                ZS[place] = mid.astype(BF)
                z_start(way, dist, half, sub, ZS.at[place])

    @pl.when(branch == core)
    def _():
        ZO[...] = PO[at_home, :]

    @pl.when(branch != core)
    def _():
        own_part.wait()

    for half in range(2):
        for sub in range(SUBS):
            cols = pl.ds((half * SUBS + sub) * width, width)
            done = ZO[:, cols].astype(F32)
            for way in range(2):
                arrived(ZF.at[way, half, sub], z_recv.at[way, 0, half, sub])
                done += ZF[way, half, sub].astype(F32)
            out[:, cols] = done.astype(BF)

    for item in sends:
        item.wait_send()
    for item in x_items:
        item.wait_send()
    for chip in range(4):
        for item in stat_copies(chip):
            item.wait_send()
    for i in range(3):
        for k in range(2):
            y_copy(i, k).wait_send()
    cross_copy.wait_send()
    swap.wait_send()
    swap_q.wait_send()
    for item in z_items:
        item.wait_send()


def per_device(queries, keys, values, reward_grad, qkv_weight):
    def vm(*shape, dtype=BF):
        return pltpu.VMEM(shape, dtype)

    dma = pltpu.SemaphoreType.DMA
    sub = FEAT // 2 // SUBS
    scratch = [
        vm(NQ, HEAD_DIM), vm(NQ, HEAD_DIM), vm(NK, HEAD_DIM), vm(NK, HEAD_DIM),
        vm(HEAD_DIM, NK), vm(NQ, HEAD_DIM), vm(NQ, HEAD_DIM),
        vm(NK, NQ), vm(NK, NQ),
        vm(PER_CHIP, NK, TILE, dtype=F32), vm(NK, NQ, dtype=F32),
        vm(3, FEAT, 2 * HEAD_DIM),
        vm(4, 8, CHIP, dtype=F32), vm(3, 4, 8, CHIP, dtype=F32), vm(4, 8, CHIP, dtype=F32),
        vm(NQ, HEAD_DIM), vm(4, 2, ROWS, HEAD_DIM),
        vm(2, 3, ROWS, HEAD_DIM), vm(3, 2, ROWS, HEAD_DIM),
        vm(ROWS, HEAD_DIM), vm(ROWS, HEAD_DIM), vm(2, 3, ROWS, HEAD_DIM),
        vm(ROWS, FEAT, dtype=F32), vm(ROWS, FEAT),
        vm(2, 4, 2, SUBS, TOK, sub), vm(2, 3, 2, SUBS, TOK, sub),
        vm(2, 2, SUBS, TOK, sub), vm(TOK, FEAT),
        dma((4, 2)), dma((4, 2)), dma((2, 2)), dma((2, 2)), dma((20,)), dma(()),
        dma((3, 4)), dma((3, 4)), dma((2, 3)), dma((2, 3)), dma((3, 2)), dma((3, 2)),
        dma(()), dma(()), dma((2,)), dma((2,)), dma((2, 4, 2, SUBS)), dma((2, 4, 2, SUBS)), dma(()), dma(()),
        pltpu.SemaphoreType.REGULAR,
    ]
    return pl.pallas_call(
        kernel,
        out_shape=jax.ShapeDtypeStruct((TOK, FEAT), BF),
        in_specs=[pl.BlockSpec(memory_space=pl.ANY)] * 5,
        out_specs=pl.BlockSpec(memory_space=pltpu.VMEM),
        scratch_shapes=scratch,
        compiler_params=pltpu.CompilerParams(
            collective_id=0, has_side_effects=True, vmem_limit_bytes=62 * 2**20
        ),
    )(queries, keys, values, reward_grad, qkv_weight)


def solution(mesh):
    placed = (
        P("branch", "blk", "head"),
        P("branch", "blk", "head"),
        P("branch", "blk", "head"),
        P("blk", "head"),
        P(None, None, "head"),
    )
    return jax.shard_map(
        per_device,
        mesh=mesh,
        in_specs=placed,
        out_specs=P(("blk", "head"), "branch"),
        check_vma=False,
    )
```
